256 devices in a mesh: half: 2 (over x_lo), row: 16 (over z, core), col: 8 (over y, x_hi).
Axes of the slice: x: 4 (x_hi: 2, x_lo: 2; x = x_hi * 2 + x_lo), y: 4, z: 8, core: 2. Of those that a mesh axis runs over, the one named last changes fastest.
Arguments:
- child_update: float32 [2, 16384, 1024], P('half', ('row', 'col')), may hold values from -4 to 4
- parent_front: float32 [32768, 4096], P(('row', 'col'), 'half'), may hold values from -4 to 192, as said below
- row_map: int32 [2, 128], P(None, ('row', 'col')), may hold values from 0 to 255, as said below
- col_map: int32 [2, 8], replicated, may hold values from 0 to 31, as said below
Outputs:
- factored: float32 [32768, 4096], P('row', ('half', 'col'))
The draws below stay inside these ranges and needn't reach their ends.
Inputs may be any that keep to these rules, and one draw needn't show every extreme that they name: parent_front's diagonal entries lie between 96 and 192. `row_map`: the blocks of the k-th run of 1024 update matrix rows name distinct parent blocks of the k-th run of 2048 parent rows, in no fixed order. `col_map`: each row holds distinct increasing block numbers.
All inputs are finite; a program needn't handle non-finite values.
Results may differ from the reference program's by a relative error of at most 0.000075.
Values sent between devices are 32-bit elements; how exact they have to be, the bound alone decides.
No kernel may reach another device: no remote copies, remote signals or barrier semaphores. Data moves between devices by JAX's collectives and lax.ppermute only.
A program may use at most 128 MiB of HBM per device.

```python
import jax
import jax.numpy as jnp
from jax import lax

BLK = 128
NB = 1024
W = 4096
KC = 1024
CROW = 128
SPAN = 2048
CSPAN = 1024
P_SIZE = 32768
MC = 16384
N_COL = 8


def draw_parent_front(key, part):
    key = jax.random.fold_in(key, 1)
    base_key, diag_key = jax.random.split(key)
    base = jnp.clip(0.8 * jax.random.normal(base_key, (P_SIZE, W), jnp.float32), -4.0, 4.0)
    diag_values = jnp.exp(jax.random.uniform(diag_key, (W,), jnp.float32, jnp.log(96.0), jnp.log(192.0)))
    row_ids = lax.broadcasted_iota(jnp.int32, (P_SIZE, W), 0)
    col_ids = lax.broadcasted_iota(jnp.int32, (P_SIZE, W), 1)
    return jnp.where(row_ids == col_ids, diag_values[None, :], base)


def draw_row_map(key, part):
    key = jax.random.fold_in(key, 2)
    groups = P_SIZE // SPAN
    group_parent = SPAN // BLK
    group_child = CSPAN // BLK
    scores = jax.random.randint(key, (2, groups, group_parent), 0, 1 << 20)
    scores = scores * group_parent + jnp.arange(group_parent, dtype=jnp.int32)[None, None, :]
    scores = scores.at[0, 0, 0].set(-1)
    scores = scores.at[1, groups - 1, group_parent - 1].set(-1)
    order = jnp.argsort(scores, axis=2, stable=True).astype(jnp.int32)
    far_slot = N_COL // 2 * (CROW // BLK)
    slot_ids = jnp.arange(group_parent, dtype=jnp.int32)[None, None, :]
    at_far = order[:, :, far_slot:far_slot + 1]
    order = jnp.where(order == 0, at_far, jnp.where(slot_ids == far_slot, 0, order))
    chosen = order[:, :, :group_child]
    blocks = chosen + (jnp.arange(groups, dtype=jnp.int32) * group_parent)[None, :, None]
    return blocks.reshape(2, groups * group_child).astype(jnp.int32)


def draw_col_map(key, part):
    key = jax.random.fold_in(key, 3)
    wblocks = W // BLK
    kblocks = KC // BLK
    result = []
    for sibling in range(2):
        order = jax.random.permutation(jax.random.fold_in(key, sibling), wblocks - 2) + 1
        chosen = jnp.concatenate([jnp.array([0, wblocks - 1], jnp.int32), order[:kblocks - 2].astype(jnp.int32)])
        result.append(jnp.sort(chosen))
    return jnp.stack(result).astype(jnp.int32)


def block_scale(stream_key, shape, shards, low, high):
    level, own = 1.0, jax.random.fold_in(stream_key, 6)
    for position, blocks in shards:
        draws = jnp.exp(jax.random.uniform(jax.random.fold_in(own, position), (blocks,), jnp.float32, low / len(shards), high / len(shards)))
        level = level * jnp.repeat(draws, shape[position] // blocks).reshape([-1 if axis == position else 1 for axis in range(len(shape))])
    return level


def gaussian(stream_key, extent, spread, most, shards=(), held_as=jnp.bfloat16):
    level = block_scale(stream_key, extent, shards, -0.22, 0.18) if shards else 1.0
    drawn = jax.random.normal(stream_key, extent, jnp.float32) * spread * level
    return jnp.minimum(jnp.maximum(drawn, -most), most).astype(held_as)


def setup_inputs(seed: int = 0) -> dict:
    keys = jax.random.split(jax.random.key(seed), 5)
    return {
        "child_update": gaussian(keys[0], (2, MC, KC), 0.5, 4.0, ((0, 2), (1, 128)), jnp.float32),
        "parent_front": draw_parent_front(jax.random.fold_in(keys[4], 71), 0),
        "row_map": draw_row_map(jax.random.fold_in(keys[4], 71), 0),
        "col_map": draw_col_map(jax.random.fold_in(keys[4], 71), 0),
    }


def reference(child_update, parent_front, row_map, col_map):
    block_offsets = jnp.arange(BLK, dtype=jnp.int32)
    front_slab = parent_front
    for sibling in range(2):
        parent_rows = (row_map[sibling][:, None] * BLK + block_offsets[None, :]).reshape(-1).astype(jnp.int32)
        parent_cols = (col_map[sibling][:, None] * BLK + block_offsets[None, :]).reshape(-1).astype(jnp.int32)
        front_slab = front_slab.at[parent_rows[:, None], parent_cols[None, :]].add(child_update[sibling])
    lower_factor = jnp.linalg.cholesky(front_slab[:NB, :NB])
    below = lax.linalg.triangular_solve(lower_factor, front_slab[NB:, :NB], left_side=False, lower=True, transpose_a=True)
    panel = jnp.concatenate([lower_factor, below], 0)
    width = parent_front.shape[1]
    trailing = front_slab[:, NB:] - jnp.dot(panel, panel[NB:width].T, precision=lax.Precision.HIGHEST)
    return jnp.concatenate([panel, trailing], 1)
```

```python
import jax
import jax.numpy as jnp
from jax import lax
from jax.experimental import pallas as pl
from jax.experimental.pallas import tpu as pltpu
from jax.sharding import PartitionSpec as P

BLK = 128
NB = 1024
W = 4096
STRIP = 64
PLANE = ("col", "half")
HIGHEST = lax.Precision.HIGHEST
VMEM_LIMIT = 48 * 1024 * 1024


def prep_kernel(src_ref, hit_ref, child_ref, parent_ref, rows_ref, strips_ref, wide_ref):
    is_first_half = rows_ref[2]
    for w in range(W // BLK):
        start = pl.multiple_of(src_ref[w] * BLK, BLK)
        block = jnp.where(hit_ref[w] > 0, child_ref[:, pl.ds(start, BLK)], 0.0)
        j = w // 2
        q = (j % 8) * 2 + j // 8
        wide_ref[q, :, (w % 2) * BLK : (w % 2 + 1) * BLK] = block
        if w < NB // BLK:
            turned = block.T
            strips_ref[2 * w, :, 0:BLK] = turned[0:STRIP]
            strips_ref[2 * w + 1, :, 0:BLK] = turned[STRIP:BLK]

    @pl.when(is_first_half == 1)
    def _():
        for w in range(NB // BLK):
            turned = parent_ref[:, w * BLK : (w + 1) * BLK].T
            strips_ref[2 * w, :, BLK : 3 * BLK] = turned[0:STRIP]
            strips_ref[2 * w + 1, :, BLK : 3 * BLK] = turned[STRIP:BLK]

    @pl.when(is_first_half != 1)
    def _():
        for s in range(2):
            value = jnp.full((STRIP, BLK), rows_ref[s], jnp.int32).astype(jnp.float32)
            for d in range(16):
                strips_ref[d, :, (1 + s) * BLK : (2 + s) * BLK] = value


def prep(child, parent, source, hit, rows):
    smem = pl.BlockSpec(memory_space=pltpu.SMEM)
    return pl.pallas_call(
        prep_kernel,
        grid=(1,),
        in_specs=[
            smem,
            smem,
            pl.BlockSpec((BLK, NB), lambda i: (0, 0)),
            pl.BlockSpec((2 * BLK, NB), lambda i: (0, 0)),
            smem,
        ],
        out_specs=[
            pl.BlockSpec((16, STRIP, 3 * BLK), lambda i: (0, 0, 0)),
            pl.BlockSpec((16, BLK, 2 * BLK), lambda i: (0, 0, 0)),
        ],
        out_shape=[
            jax.ShapeDtypeStruct((16, STRIP, 3 * BLK), jnp.float32),
            jax.ShapeDtypeStruct((16, BLK, 2 * BLK), jnp.float32),
        ],
        compiler_params=pltpu.CompilerParams(vmem_limit_bytes=VMEM_LIMIT),
        name="prep",
    )(source, hit, child, parent, rows)


def strip_kernel(where_ref, pieces_ref, out_ref):
    for c in range(8):
        out_ref[:, 256 * c : 256 * (c + 1)] = pieces_ref[2 * c, :, BLK : 3 * BLK]
    for c in range(8):
        for s in range(2):
            at = pl.multiple_of(where_ref[s, c] * BLK, BLK)
            out_ref[:, pl.ds(at, BLK)] += pieces_ref[2 * c + s, :, 0:BLK]


def assemble_strip(pieces, where):
    return pl.pallas_call(
        strip_kernel,
        in_specs=[pl.BlockSpec(memory_space=pltpu.SMEM), pl.BlockSpec(memory_space=pltpu.VMEM)],
        out_specs=pl.BlockSpec(memory_space=pltpu.VMEM),
        out_shape=jax.ShapeDtypeStruct((STRIP, 2048), jnp.float32),
        compiler_params=pltpu.CompilerParams(vmem_limit_bytes=VMEM_LIMIT),
        name="strip",
    )(where, pieces)


def split_bf16(x):
    high = x.astype(jnp.bfloat16)
    return high, (x - high.astype(jnp.float32)).astype(jnp.bfloat16)


def product_kernel(inv_ref, flags_ref, wt_ref, rows_ref, sym_ref, front_ref, child_ref, out_ref, wh, wl):
    t = pl.program_id(0)

    @pl.when(t == 0)
    def _():
        high, low = split_bf16(wt_ref[...])
        wh[...] = high
        wl[...] = low

    use_sym = jnp.logical_and(flags_ref[0] == 1, t < 4)
    a = jnp.where(use_sym, sym_ref[...], rows_ref[...])
    ah, al = split_bf16(a)
    dims = (((1,), (0,)), ((), ()))

    def dot(x, y):
        return lax.dot_general(x, y, dims, preferred_element_type=jnp.float32)

    turned = dot(wh[...], ah) + (dot(wh[...], al) + dot(wl[...], ah))
    term = turned.T
    keep = flags_ref[1] == 0
    for b in range(2):
        base = front_ref[b * BLK : (b + 1) * BLK, :]
        for s in range(2):
            k = inv_ref[s, 2 * t + b]
            part = child_ref[jnp.maximum(k, 0) * 2 + s]
            base = base + jnp.where(k >= 0, part, 0.0)
        base = jnp.where(keep, base, 0.0)
        out_ref[b * BLK : (b + 1) * BLK, :] = base - term[b * BLK : (b + 1) * BLK, :]


def product(inv, flags, wt, rows, sym, front, child):
    smem = pl.BlockSpec(memory_space=pltpu.SMEM)
    return pl.pallas_call(
        product_kernel,
        grid=(8,),
        in_specs=[
            smem,
            smem,
            pl.BlockSpec((256, NB), lambda t: (0, 0)),
            pl.BlockSpec((NB, 256), lambda t: (0, t)),
            pl.BlockSpec((NB, 256), lambda t: (0, jnp.minimum(t, 3))),
            pl.BlockSpec((256, 256), lambda t: (t, 0)),
            pl.BlockSpec((16, BLK, 256), lambda t: (0, 0, 0)),
        ],
        out_specs=pl.BlockSpec((256, 256), lambda t: (t, 0)),
        out_shape=jax.ShapeDtypeStruct((2048, 256), jnp.float32),
        scratch_shapes=[pltpu.VMEM((256, NB), jnp.bfloat16), pltpu.VMEM((256, NB), jnp.bfloat16)],
        compiler_params=pltpu.CompilerParams(vmem_limit_bytes=VMEM_LIMIT),
        cost_estimate=pl.CostEstimate(flops=3 * 2 * 2048 * 1024 * 256, bytes_accessed=16 << 20, transcendentals=0),
        name="product",
    )(inv, flags, wt, rows, sym, front, child)


def body(child_update, parent_front, row_map, col_map):
    half = lax.axis_index("half")
    row = lax.axis_index("row")
    col = lax.axis_index("col")
    strip = half * 8 + col
    targets = jnp.arange(W // BLK, dtype=jnp.int32)
    own_columns = lax.dynamic_index_in_dim(col_map, half, 0, keepdims=False)
    match = (own_columns[:, None] == targets[None, :]).astype(jnp.int32)
    source = jnp.sum(match * jnp.arange(8, dtype=jnp.int32)[:, None], 0)
    hit = jnp.sum(match, 0)
    rows = jnp.concatenate([row_map[:, 0] - row * 16, jnp.where(half == 0, 1, 0)[None]]).astype(jnp.int32)
    strips, wide = prep(child_update[0], parent_front, source, hit, rows)

    pieces = lax.all_to_all(strips, PLANE, 0, 0, tiled=True)
    where = pieces[1::2, 0, BLK : 3 * BLK : BLK].T.astype(jnp.int32)
    a_strip = assemble_strip(pieces, where)

    diag_strip = a_strip[:, :NB]
    core0 = [lax.ppermute(diag_strip, "row", [(0, 2 * z)]) for z in range(1, 8)]
    spread = jnp.where(row == 0, diag_strip, sum(core0[1:], core0[0]))
    is_core0 = row % 2 == 0
    to_core1 = lax.ppermute(spread[STRIP // 2 :], "row", [(2 * z, 2 * z + 1) for z in range(8)])
    mine = jnp.where(is_core0, spread[: STRIP // 2], to_core1)
    gathered = lax.all_to_all(
        jnp.broadcast_to(mine[None], (16, STRIP // 2, NB)), PLANE, 0, 0, tiled=True
    )
    other = lax.ppermute(gathered, "row", [(i, i ^ 1) for i in range(16)])
    first = jnp.where(is_core0, gathered, other)
    second = jnp.where(is_core0, other, gathered)
    diag = jnp.concatenate([first, second], 1).reshape(NB, NB)

    wanted = jnp.broadcast_to(
        a_strip.reshape(STRIP, 8, 1, 256).transpose(1, 2, 0, 3), (8, 2, STRIP, 256)
    ).reshape(16, STRIP, 256)
    matching = lax.all_to_all(wanted, PLANE, 0, 0, tiled=True).reshape(NB, 256)
    sent = [
        lax.ppermute(matching, ("half", "row"), [(0, 2 * z), (16 + 1, 16 + 2 * z + 1)]) for z in range(1, 8)
    ]
    spread_c = jnp.where(row < 2, matching, sum(sent[1:], sent[0]))
    swapped = lax.ppermute(
        spread_c,
        ("half", "row"),
        [(2 * z, 2 * z + 1) for z in range(8)] + [(16 + 2 * z + 1, 16 + 2 * z) for z in range(8)],
    )
    c_turned = jnp.where(row % 2 == half, spread_c, swapped)

    a_turned = lax.all_gather(a_strip, PLANE, axis=0, tiled=True)
    front = lax.all_to_all(parent_front, "col", split_axis=1, concat_axis=0, tiled=True)
    child = lax.all_to_all(wide, PLANE, 0, 0, tiled=True)

    sym = (diag + diag.T) * 0.5
    lower = lax.linalg.cholesky(sym, symmetrize_input=False)
    solved = lax.linalg.triangular_solve(lower, c_turned, left_side=True, lower=True)
    unit = (
        jnp.arange(NB, dtype=jnp.int32)[:, None] == strip * 256 + jnp.arange(256, dtype=jnp.int32)[None, :]
    ).astype(jnp.float32)
    is_panel = strip < 4
    middle = jnp.where(is_panel, -unit, solved)
    wt = lax.linalg.triangular_solve(lower, middle, left_side=True, lower=True, transpose_a=True).T

    blocks = jnp.arange(16, dtype=jnp.int32)
    order = jnp.arange(8, dtype=jnp.int32)
    inv = jnp.max(jnp.where(where[:, :, None] == blocks[None, None, :], order[None, :, None], -1), axis=1)
    flags = jnp.stack([(row == 0).astype(jnp.int32), is_panel.astype(jnp.int32)])
    return product(inv, flags, wt, a_turned, sym, front, child)


def solution(mesh):
    return jax.shard_map(
        body,
        mesh=mesh,
        in_specs=(
            P("half", ("row", "col"), None),
            P(("row", "col"), "half"),
            P(None, ("row", "col")),
            P(),
        ),
        out_specs=P("row", ("half", "col")),
        check_vma=False,
    )
```

```python
import jax
import jax.numpy as jnp
from jax import lax
from jax.experimental import pallas as pl
from jax.experimental.pallas import tpu as pltpu
from jax.sharding import PartitionSpec as P

BLK = 128
NB = 1024
W = 4096
STRIP = 64
PLANE = ("col", "half")
VMEM_LIMIT = 56 * 1024 * 1024


def prep_kernel(src_ref, hit_ref, child_ref, parent_ref, rows_ref, strips_ref, wide_ref):
    is_first_half = rows_ref[2]
    for w in range(W // BLK):
        start = pl.multiple_of(src_ref[w] * BLK, BLK)
        block = jnp.where(hit_ref[w] > 0, child_ref[:, pl.ds(start, BLK)], 0.0)
        j = w // 2
        q = (j % 8) * 2 + j // 8
        wide_ref[q, :, (w % 2) * BLK : (w % 2 + 1) * BLK] = block
        if w < NB // BLK:
            turned = block.T
            strips_ref[2 * w, :, 0:BLK] = turned[0:STRIP]
            strips_ref[2 * w + 1, :, 0:BLK] = turned[STRIP:BLK]

    @pl.when(is_first_half == 1)
    def _():
        for w in range(NB // BLK):
            turned = parent_ref[:, w * BLK : (w + 1) * BLK].T
            strips_ref[2 * w, :, BLK : 3 * BLK] = turned[0:STRIP]
            strips_ref[2 * w + 1, :, BLK : 3 * BLK] = turned[STRIP:BLK]

    @pl.when(is_first_half != 1)
    def _():
        for s in range(2):
            value = jnp.full((STRIP, BLK), rows_ref[s], jnp.int32).astype(jnp.float32)
            for d in range(16):
                strips_ref[d, :, (1 + s) * BLK : (2 + s) * BLK] = value


def prep(child, parent, source, hit, rows):
    smem = pl.BlockSpec(memory_space=pltpu.SMEM)
    return pl.pallas_call(
        prep_kernel,
        grid=(1,),
        in_specs=[
            smem,
            smem,
            pl.BlockSpec((BLK, NB), lambda i: (0, 0)),
            pl.BlockSpec((2 * BLK, NB), lambda i: (0, 0)),
            smem,
        ],
        out_specs=[
            pl.BlockSpec((16, STRIP, 3 * BLK), lambda i: (0, 0, 0)),
            pl.BlockSpec((16, BLK, 2 * BLK), lambda i: (0, 0, 0)),
        ],
        out_shape=[
            jax.ShapeDtypeStruct((16, STRIP, 3 * BLK), jnp.float32),
            jax.ShapeDtypeStruct((16, BLK, 2 * BLK), jnp.float32),
        ],
        compiler_params=pltpu.CompilerParams(vmem_limit_bytes=VMEM_LIMIT),
        name="prep",
    )(source, hit, child, parent, rows)


def strip_kernel(where_ref, pieces_ref, out_ref):
    for c in range(8):
        out_ref[:, 256 * c : 256 * (c + 1)] = pieces_ref[2 * c, :, BLK : 3 * BLK]
    for c in range(8):
        for s in range(2):
            at = pl.multiple_of(where_ref[s, c] * BLK, BLK)
            out_ref[:, pl.ds(at, BLK)] += pieces_ref[2 * c + s, :, 0:BLK]


def assemble_strip(pieces, where):
    return pl.pallas_call(
        strip_kernel,
        in_specs=[pl.BlockSpec(memory_space=pltpu.SMEM), pl.BlockSpec(memory_space=pltpu.VMEM)],
        out_specs=pl.BlockSpec(memory_space=pltpu.VMEM),
        out_shape=jax.ShapeDtypeStruct((STRIP, 2048), jnp.float32),
        compiler_params=pltpu.CompilerParams(vmem_limit_bytes=VMEM_LIMIT),
        name="strip",
    )(where, pieces)


def split_bf16(x):
    high = x.astype(jnp.bfloat16)
    return high, (x - high.astype(jnp.float32)).astype(jnp.bfloat16)


def dot3(xh, xl, yh, yl):
    def dot(x, y):
        return lax.dot_general(x, y, (((1,), (0,)), ((), ())), preferred_element_type=jnp.float32)

    return dot(xh, yh) + (dot(xh, yl) + dot(xl, yh))


def lane(x, i):
    return jnp.broadcast_to(x[:, i : i + 1], (8, BLK))


def sub(x, i):
    return jnp.broadcast_to(x[i : i + 1, :], (8, x.shape[1]))


def eliminate(d, e, base):
    groups = len(d)
    place = lax.broadcasted_iota(jnp.int32, (8, BLK), 0)
    for g in range(groups):
        first = base + 8 * g
        columns = [lane(d[g], first + i) for i in range(8)]
        below = [[lane(d[n], first + i) for i in range(8)] for n in range(g + 1, groups)]
        scales = jnp.zeros((8, BLK), jnp.float32)
        for i in range(8):
            r = lax.rsqrt(sub(columns[i], i))
            scales = jnp.where(place == i, r, scales)
            l = columns[i] * r
            low = [b[i] * r for b in below]
            for m in range(i + 1, 8):
                f = sub(l, m)
                columns[m] = columns[m] - l * f
                for n, b in enumerate(below):
                    b[m] = b[m] - low[n] * f
            dr = sub(d[g], i) * r
            er = sub(e[g], i) * r
            masked = jnp.where(place > i, l, 0.0)
            d[g] = d[g] - masked * dr
            e[g] = e[g] - masked * er
            for n in range(len(below)):
                d[g + 1 + n] = d[g + 1 + n] - low[n] * dr
                e[g + 1 + n] = e[g + 1 + n] - low[n] * er
        d[g] = d[g] * scales
        e[g] = e[g] * scales
    return d, e


GROUP = 32


def factor_block(de_ref):
    for p in range(BLK // GROUP):
        base = p * GROUP
        rows = [slice(base + 8 * g, base + 8 * g + 8) for g in range(GROUP // 8)]
        d = [de_ref[r, 0:BLK] for r in rows]
        e = [de_ref[r, BLK : 2 * BLK] for r in rows]
        d, e = eliminate(d, e, base)
        for r, x, y in zip(rows, d, e):
            de_ref[r, 0:BLK] = x
            de_ref[r, BLK : 2 * BLK] = y
        if base + GROUP < BLK:
            done = de_ref[base : base + GROUP, :]
            left = done[:, 0:BLK].T[base + GROUP :]
            lh, ll = split_bf16(left)
            rh, rl = split_bf16(done)
            de_ref[base + GROUP :, :] -= dot3(lh, ll, rh, rl)


def solve_kernel(flags_ref, own_ref, other_ref, c_ref, wt_ref, sym_ref, lh, ll, uh, ul, mh, ml, yh, yl, de, row):
    core = flags_ref[0]
    strip = flags_ref[1]
    blocks = NB // BLK
    for q in range(16):
        at = pl.multiple_of(q * STRIP + core * 32, 32)
        sym_ref[pl.ds(at, 32), :] = own_ref[q]
        at = pl.multiple_of(q * STRIP + (1 - core) * 32, 32)
        sym_ref[pl.ds(at, 32), :] = other_ref[q]
    for i in range(blocks):
        for j in range(i, blocks):
            a = sym_ref[i * BLK : (i + 1) * BLK, j * BLK : (j + 1) * BLK]
            b = sym_ref[j * BLK : (j + 1) * BLK, i * BLK : (i + 1) * BLK]
            s = (a + b.T) * 0.5
            sym_ref[i * BLK : (i + 1) * BLK, j * BLK : (j + 1) * BLK] = s
            if j > i:
                sym_ref[j * BLK : (j + 1) * BLK, i * BLK : (i + 1) * BLK] = s.T
    mh[...] = jnp.zeros_like(mh)
    ml[...] = jnp.zeros_like(ml)
    eye = (
        lax.broadcasted_iota(jnp.int32, (BLK, BLK), 0) == lax.broadcasted_iota(jnp.int32, (BLK, BLK), 1)
    ).astype(jnp.float32)

    def step(k, _):
        for kk in range(blocks):

            @pl.when(k == kk)
            def _(kk=kk):
                here = slice(kk * BLK, (kk + 1) * BLK)
                done = kk * BLK
                up = NB - done
                if kk == 0:
                    row[:, 0:NB] = sym_ref[here, :]
                    row[:, NB:] = c_ref[here, :]
                else:
                    a, b = lh[here, 0:done], ll[here, 0:done]
                    row[:, 0:up] = sym_ref[here, done:] - dot3(a, b, uh[0:done, done:], ul[0:done, done:])
                    row[:, up:NB] = -dot3(a, b, mh[0:done, 0:done], ml[0:done, 0:done])
                    row[:, NB:] = c_ref[here, :] - dot3(a, b, yh[0:done, :], yl[0:done, :])

        de[:, 0:BLK] = row[:, 0:BLK]
        de[:, BLK:] = eye
        factor_block(de)
        ih, il = split_bf16(de[:, BLK:])
        rh, rl = split_bf16(row[:, BLK:])
        scaled = dot3(ih, il, rh, rl)
        sh, sl = split_bf16(scaled)
        for kk in range(blocks):

            @pl.when(k == kk)
            def _(kk=kk):
                here = slice(kk * BLK, (kk + 1) * BLK)
                after = (kk + 1) * BLK
                up = NB - after
                if up:
                    uh[here, after:] = sh[:, 0:up]
                    ul[here, after:] = sl[:, 0:up]
                    th, tl = split_bf16(scaled[:, 0:up].T)
                    lh[after:, here] = th
                    ll[after:, here] = tl
                if kk:
                    mh[here, 0 : kk * BLK] = sh[:, up : NB - BLK]
                    ml[here, 0 : kk * BLK] = sl[:, up : NB - BLK]
                mh[here, here] = ih
                ml[here, here] = il
                yh[here, :] = sh[:, NB - BLK :]
                yl[here, :] = sl[:, NB - BLK :]

        return 0

    lax.fori_loop(0, blocks, step, 0)

    @pl.when(strip < 4)
    def _():
        at = pl.multiple_of(jnp.minimum(strip, 3) * 256, 256)
        wt_ref[...] = -(mh[pl.ds(at, 256), :].astype(jnp.float32) + ml[pl.ds(at, 256), :].astype(jnp.float32))

    @pl.when(strip >= 4)
    def _():
        th, tl = yh[...].astype(jnp.float32).T.astype(jnp.bfloat16), yl[...].astype(jnp.float32).T.astype(jnp.bfloat16)
        for n in range(4):
            at = 256 * n
            wt_ref[:, at : at + 256] = dot3(
                th[:, at:], tl[:, at:], mh[at:, at : at + 256], ml[at:, at : at + 256]
            )


def solve(flags, own, other, c_turned):
    vmem = pl.BlockSpec(memory_space=pltpu.VMEM)
    half = pltpu.VMEM((NB, NB), jnp.bfloat16)
    return pl.pallas_call(
        solve_kernel,
        in_specs=[pl.BlockSpec(memory_space=pltpu.SMEM), vmem, vmem, vmem],
        out_specs=[vmem, vmem],
        out_shape=[jax.ShapeDtypeStruct((256, NB), jnp.float32), jax.ShapeDtypeStruct((NB, NB), jnp.float32)],
        scratch_shapes=[half] * 6
        + [pltpu.VMEM((NB, 256), jnp.bfloat16)] * 2
        + [pltpu.VMEM((BLK, 2 * BLK), jnp.float32), pltpu.VMEM((BLK, NB + 256), jnp.float32)],
        compiler_params=pltpu.CompilerParams(vmem_limit_bytes=VMEM_LIMIT),
        cost_estimate=pl.CostEstimate(flops=50_000_000_000, bytes_accessed=12 << 20, transcendentals=0),
        name="solve",
    )(flags, own, other, c_turned)


def product_kernel(inv_ref, flags_ref, wt_ref, rows_ref, sym_ref, front_ref, child_ref, out_ref, wh, wl):
    t = pl.program_id(0)

    @pl.when(t == 0)
    def _():
        high, low = split_bf16(wt_ref[...])
        wh[...] = high
        wl[...] = low

    use_sym = jnp.logical_and(flags_ref[0] == 1, t < 4)
    a = jnp.where(use_sym, sym_ref[...], rows_ref[...])
    ah, al = split_bf16(a)
    dims = (((1,), (0,)), ((), ()))

    def dot(x, y):
        return lax.dot_general(x, y, dims, preferred_element_type=jnp.float32)

    turned = dot(wh[...], ah) + (dot(wh[...], al) + dot(wl[...], ah))
    term = turned.T
    keep = flags_ref[1] == 0
    for b in range(2):
        base = front_ref[b * BLK : (b + 1) * BLK, :]
        for s in range(2):
            k = inv_ref[s, 2 * t + b]
            part = child_ref[jnp.maximum(k, 0) * 2 + s]
            base = base + jnp.where(k >= 0, part, 0.0)
        base = jnp.where(keep, base, 0.0)
        out_ref[b * BLK : (b + 1) * BLK, :] = base - term[b * BLK : (b + 1) * BLK, :]


def product(inv, flags, wt, rows, sym, front, child):
    smem = pl.BlockSpec(memory_space=pltpu.SMEM)
    return pl.pallas_call(
        product_kernel,
        grid=(8,),
        in_specs=[
            smem,
            smem,
            pl.BlockSpec((256, NB), lambda t: (0, 0)),
            pl.BlockSpec((NB, 256), lambda t: (0, t)),
            pl.BlockSpec((NB, 256), lambda t: (0, jnp.minimum(t, 3))),
            pl.BlockSpec((256, 256), lambda t: (t, 0)),
            pl.BlockSpec((16, BLK, 256), lambda t: (0, 0, 0)),
        ],
        out_specs=pl.BlockSpec((256, 256), lambda t: (t, 0)),
        out_shape=jax.ShapeDtypeStruct((2048, 256), jnp.float32),
        scratch_shapes=[pltpu.VMEM((256, NB), jnp.bfloat16), pltpu.VMEM((256, NB), jnp.bfloat16)],
        compiler_params=pltpu.CompilerParams(vmem_limit_bytes=VMEM_LIMIT),
        cost_estimate=pl.CostEstimate(flops=3 * 2 * 2048 * 1024 * 256, bytes_accessed=16 << 20, transcendentals=0),
        name="product",
    )(inv, flags, wt, rows, sym, front, child)


def body(child_update, parent_front, row_map, col_map):
    half = lax.axis_index("half")
    row = lax.axis_index("row")
    col = lax.axis_index("col")
    strip = half * 8 + col
    targets = jnp.arange(W // BLK, dtype=jnp.int32)
    own_columns = lax.dynamic_index_in_dim(col_map, half, 0, keepdims=False)
    match = (own_columns[:, None] == targets[None, :]).astype(jnp.int32)
    source = jnp.sum(match * jnp.arange(8, dtype=jnp.int32)[:, None], 0)
    hit = jnp.sum(match, 0)
    rows = jnp.concatenate([row_map[:, 0] - row * 16, jnp.where(half == 0, 1, 0)[None]]).astype(jnp.int32)
    strips, wide = prep(child_update[0], parent_front, source, hit, rows)

    pieces = lax.all_to_all(strips, PLANE, 0, 0, tiled=True)
    where = pieces[1::2, 0, BLK : 3 * BLK : BLK].T.astype(jnp.int32)
    a_strip = assemble_strip(pieces, where)

    diag_strip = a_strip[:, :NB]
    core0 = [lax.ppermute(diag_strip, "row", [(0, 2 * z)]) for z in range(1, 8)]
    spread = jnp.where(row == 0, diag_strip, sum(core0[1:], core0[0]))
    is_core0 = row % 2 == 0
    to_core1 = lax.ppermute(spread[STRIP // 2 :], "row", [(2 * z, 2 * z + 1) for z in range(8)])
    mine = jnp.where(is_core0, spread[: STRIP // 2], to_core1)
    gathered = lax.all_to_all(
        jnp.broadcast_to(mine[None], (16, STRIP // 2, NB)), PLANE, 0, 0, tiled=True
    )
    other = lax.ppermute(gathered, "row", [(i, i ^ 1) for i in range(16)])
    wanted = jnp.broadcast_to(
        a_strip.reshape(STRIP, 8, 1, 256).transpose(1, 2, 0, 3), (8, 2, STRIP, 256)
    ).reshape(16, STRIP, 256)
    matching = lax.all_to_all(wanted, PLANE, 0, 0, tiled=True).reshape(NB, 256)
    sent = [
        lax.ppermute(matching, ("half", "row"), [(0, 2 * z), (16 + 1, 16 + 2 * z + 1)]) for z in range(1, 8)
    ]
    spread_c = jnp.where(row < 2, matching, sum(sent[1:], sent[0]))
    swapped = lax.ppermute(
        spread_c,
        ("half", "row"),
        [(2 * z, 2 * z + 1) for z in range(8)] + [(16 + 2 * z + 1, 16 + 2 * z) for z in range(8)],
    )
    c_turned = jnp.where(row % 2 == half, spread_c, swapped)

    a_turned = lax.all_gather(a_strip, PLANE, axis=0, tiled=True)
    front = lax.all_to_all(parent_front, "col", split_axis=1, concat_axis=0, tiled=True)
    child = lax.all_to_all(wide, PLANE, 0, 0, tiled=True)

    place = jnp.stack([row % 2, strip]).astype(jnp.int32)
    wt, sym = solve(place, gathered, other, c_turned)

    blocks = jnp.arange(16, dtype=jnp.int32)
    order = jnp.arange(8, dtype=jnp.int32)
    inv = jnp.max(jnp.where(where[:, :, None] == blocks[None, None, :], order[None, :, None], -1), axis=1)
    flags = jnp.stack([(row == 0).astype(jnp.int32), (strip < 4).astype(jnp.int32)])
    return product(inv, flags, wt, a_turned, sym, front, child)


def solution(mesh):
    return jax.shard_map(
        body,
        mesh=mesh,
        in_specs=(
            P("half", ("row", "col"), None),
            P(("row", "col"), "half"),
            P(None, ("row", "col")),
            P(),
        ),
        out_specs=P("row", ("half", "col")),
        check_vma=False,
    )
```

```python
import jax
import jax.numpy as jnp
from jax import lax
from jax.experimental import pallas as pl
from jax.experimental.pallas import tpu as pltpu
from jax.sharding import PartitionSpec as P

BLK = 128
NB = 1024
W = 4096
STRIP = 64
RUN = 32
HALF = NB // 2
TILE = 256
PLANE = ("col", "half")
VMEM_LIMIT = 24 * 1024 * 1024


def prep_kernel(src_ref, hit_ref, child_ref, parent_ref, rows_ref, strips_ref, wide_ref):
    is_first_half = rows_ref[2]
    for w in range(W // BLK):
        start = pl.multiple_of(src_ref[w] * BLK, BLK)
        block = jnp.where(hit_ref[w] > 0, child_ref[:, pl.ds(start, BLK)], 0.0)
        j = w // 2
        q = (j % 8) * 2 + j // 8
        wide_ref[q, :, (w % 2) * BLK : (w % 2 + 1) * BLK] = block
        if w < NB // BLK:
            turned = block.T
            strips_ref[2 * w, :, 0:BLK] = turned[0:STRIP]
            strips_ref[2 * w + 1, :, 0:BLK] = turned[STRIP:BLK]

    @pl.when(is_first_half == 1)
    def _():
        for w in range(NB // BLK):
            turned = parent_ref[:, w * BLK : (w + 1) * BLK].T
            strips_ref[2 * w, :, BLK : 3 * BLK] = turned[0:STRIP]
            strips_ref[2 * w + 1, :, BLK : 3 * BLK] = turned[STRIP:BLK]

    @pl.when(is_first_half != 1)
    def _():
        for s in range(2):
            value = jnp.full((STRIP, BLK), rows_ref[s], jnp.int32).astype(jnp.float32)
            for d in range(16):
                strips_ref[d, :, (1 + s) * BLK : (2 + s) * BLK] = value


def prep(child, parent, source, hit, rows):
    smem = pl.BlockSpec(memory_space=pltpu.SMEM)
    return pl.pallas_call(
        prep_kernel,
        grid=(1,),
        in_specs=[
            smem,
            smem,
            pl.BlockSpec((BLK, NB), lambda i: (0, 0)),
            pl.BlockSpec((2 * BLK, NB), lambda i: (0, 0)),
            smem,
        ],
        out_specs=[
            pl.BlockSpec((16, STRIP, 3 * BLK), lambda i: (0, 0, 0)),
            pl.BlockSpec((16, BLK, 2 * BLK), lambda i: (0, 0, 0)),
        ],
        out_shape=[
            jax.ShapeDtypeStruct((16, STRIP, 3 * BLK), jnp.float32),
            jax.ShapeDtypeStruct((16, BLK, 2 * BLK), jnp.float32),
        ],
        compiler_params=pltpu.CompilerParams(vmem_limit_bytes=VMEM_LIMIT),
        name="prep",
    )(source, hit, child, parent, rows)


def strip_kernel(where_ref, place_ref, pieces_ref, out_ref, keep_ref, give_ref):
    core = place_ref[0]
    for c in range(8):
        out_ref[:, 256 * c : 256 * (c + 1)] = pieces_ref[2 * c, :, BLK : 3 * BLK]
    for c in range(8):
        for s in range(2):
            at = pl.multiple_of(where_ref[s, c] * BLK, BLK)
            out_ref[:, pl.ds(at, BLK)] += pieces_ref[2 * c + s, :, 0:BLK]
    keep_ref[...] = out_ref[pl.ds(pl.multiple_of(core * RUN, RUN), RUN), :]
    give_ref[...] = out_ref[pl.ds(pl.multiple_of((1 - core) * RUN, RUN), RUN), :]


def assemble_strip(pieces, where, place):
    smem = pl.BlockSpec(memory_space=pltpu.SMEM)
    vmem = pl.BlockSpec(memory_space=pltpu.VMEM)
    half = jax.ShapeDtypeStruct((RUN, 2048), jnp.float32)
    return pl.pallas_call(
        strip_kernel,
        in_specs=[smem, smem, vmem],
        out_specs=[vmem] * 3,
        out_shape=[jax.ShapeDtypeStruct((STRIP, 2048), jnp.float32), half, half],
        compiler_params=pltpu.CompilerParams(vmem_limit_bytes=24 * 1024 * 1024),
        name="strip",
    )(where, place, pieces)


def share_kernel(place_ref, keep_ref, got_ref, start_ref, wanted_ref):
    core = place_ref[0]
    start_ref[...] = jnp.where(core == 0, keep_ref[:, 0:NB], got_ref[:, 0:NB])
    for c in range(8):
        a = keep_ref[:, 256 * c : 256 * (c + 1)]
        b = got_ref[:, 256 * c : 256 * (c + 1)]
        wanted_ref[2 * c] = jnp.where(core == 0, a, b)
        wanted_ref[2 * c + 1] = jnp.where(core == 0, b, a)


def share(place, keep, got):
    vmem = pl.BlockSpec(memory_space=pltpu.VMEM)
    return pl.pallas_call(
        share_kernel,
        in_specs=[pl.BlockSpec(memory_space=pltpu.SMEM), vmem, vmem],
        out_specs=[vmem] * 2,
        out_shape=[
            jax.ShapeDtypeStruct((RUN, NB), jnp.float32),
            jax.ShapeDtypeStruct((16, RUN, 256), jnp.float32),
        ],
        compiler_params=pltpu.CompilerParams(vmem_limit_bytes=16 * 1024 * 1024),
        name="share",
    )(place, keep, got)


def turn_kernel(parent_ref, out_ref):
    for n in range(8):
        out_ref[n] = parent_ref[:, 256 * n : 256 * (n + 1)]


def turn(parent):
    vmem = pl.BlockSpec(memory_space=pltpu.VMEM)
    return pl.pallas_call(
        turn_kernel,
        in_specs=[vmem],
        out_specs=vmem,
        out_shape=jax.ShapeDtypeStruct((8, 256, 256), jnp.float32),
        compiler_params=pltpu.CompilerParams(vmem_limit_bytes=16 * 1024 * 1024),
        cost_estimate=pl.CostEstimate(flops=60_000_000_000, bytes_accessed=4 << 20, transcendentals=0),
        name="turn",
    )(parent)


def pick_kernel(copies, index_ref, *refs):
    out_ref = refs[-1]
    for i in range(len(refs) - 1):

        @pl.when(index_ref[0] == i)
        def _(i=i):
            if copies:
                for n in range(copies):
                    out_ref[n] = refs[i][...]
            else:
                out_ref[...] = refs[i][...]


def pick(index, arrays, copies=0):
    shape = arrays[0].shape
    vmem = pl.BlockSpec(memory_space=pltpu.VMEM)
    return pl.pallas_call(
        lambda *refs: pick_kernel(copies, *refs),
        in_specs=[pl.BlockSpec(memory_space=pltpu.SMEM)] + [vmem] * len(arrays),
        out_specs=vmem,
        out_shape=jax.ShapeDtypeStruct((copies,) + shape if copies else shape, arrays[0].dtype),
        compiler_params=pltpu.CompilerParams(vmem_limit_bytes=16 * 1024 * 1024),
        name="pick",
    )(index, *arrays)


def split_bf16(x):
    high = x.astype(jnp.bfloat16)
    return high, (x - high.astype(jnp.float32)).astype(jnp.bfloat16)


def dot3(xh, xl, yh, yl):
    def dot(x, y):
        return lax.dot_general(x, y, (((1,), (0,)), ((), ())), preferred_element_type=jnp.float32)

    return dot(xh, yh) + (dot(xh, yl) + dot(xl, yh))


def lane(x, i):
    return jnp.broadcast_to(x[:, i : i + 1], (8, BLK))


def sub(x, i):
    return jnp.broadcast_to(x[i : i + 1, :], (8, x.shape[1]))


def eliminate(d, e, base):
    groups = len(d)
    place = lax.broadcasted_iota(jnp.int32, (8, BLK), 0)
    for g in range(groups):
        first = base + 8 * g
        columns = [lane(d[g], first + i) for i in range(8)]
        below = [[lane(d[n], first + i) for i in range(8)] for n in range(g + 1, groups)]
        scales = jnp.zeros((8, BLK), jnp.float32)
        for i in range(8):
            r = lax.rsqrt(sub(columns[i], i))
            scales = jnp.where(place == i, r, scales)
            l = columns[i] * r
            low = [b[i] * r for b in below]
            for m in range(i + 1, 8):
                f = sub(l, m)
                columns[m] = columns[m] - l * f
                for n, b in enumerate(below):
                    b[m] = b[m] - low[n] * f
            dr = sub(d[g], i) * r
            er = sub(e[g], i) * r
            masked = jnp.where(place > i, l, 0.0)
            d[g] = d[g] - masked * dr
            e[g] = e[g] - masked * er
            for n in range(len(below)):
                d[g + 1 + n] = d[g + 1 + n] - low[n] * dr
                e[g + 1 + n] = e[g + 1 + n] - low[n] * er
        d[g] = d[g] * scales
        e[g] = e[g] * scales
    return d, e


GROUP = 32


def factor_block(de_ref):
    for p in range(BLK // GROUP):
        base = p * GROUP
        rows = [slice(base + 8 * g, base + 8 * g + 8) for g in range(GROUP // 8)]
        d = [de_ref[r, 0:BLK] for r in rows]
        e = [de_ref[r, BLK : 2 * BLK] for r in rows]
        d, e = eliminate(d, e, base)
        for r, x, y in zip(rows, d, e):
            de_ref[r, 0:BLK] = x
            de_ref[r, BLK : 2 * BLK] = y
        if base + GROUP < BLK:
            done = de_ref[base : base + GROUP, :]
            left = done[:, 0:BLK].T[base + GROUP :]
            lh, ll = split_bf16(left)
            rh, rl = split_bf16(done)
            de_ref[base + GROUP :, :] -= dot3(lh, ll, rh, rl)


def factor_half(a_ref, r_ref, lh, ll, uh, ul, mh, ml, zh, zl, de, row):
    blocks = HALF // BLK
    mh[...] = jnp.zeros_like(mh)
    ml[...] = jnp.zeros_like(ml)
    eye = (
        lax.broadcasted_iota(jnp.int32, (BLK, BLK), 0) == lax.broadcasted_iota(jnp.int32, (BLK, BLK), 1)
    ).astype(jnp.float32)

    def step(k, _):
        for kk in range(blocks):

            @pl.when(k == kk)
            def _(kk=kk):
                here = slice(kk * BLK, (kk + 1) * BLK)
                done = kk * BLK
                up = HALF - done
                if kk == 0:
                    row[:, 0:HALF] = a_ref[here, 0:HALF]
                    row[:, HALF:] = r_ref[here, :]
                else:
                    x, y = lh[here, 0:done], ll[here, 0:done]
                    row[:, 0:up] = a_ref[here, done:HALF] - dot3(x, y, uh[0:done, done:], ul[0:done, done:])
                    row[:, up:HALF] = -dot3(x, y, mh[0:done, 0:done], ml[0:done, 0:done])
                    row[:, HALF:] = r_ref[here, :] - dot3(x, y, zh[0:done, :], zl[0:done, :])

        de[:, 0:BLK] = row[:, 0:BLK]
        de[:, BLK:] = eye
        factor_block(de)
        ih, il = split_bf16(de[:, BLK:])
        rh, rl = split_bf16(row[:, BLK:])
        scaled = dot3(ih, il, rh, rl)
        sh, sl = split_bf16(scaled)
        for kk in range(blocks):

            @pl.when(k == kk)
            def _(kk=kk):
                here = slice(kk * BLK, (kk + 1) * BLK)
                after = (kk + 1) * BLK
                up = HALF - after
                if up:
                    uh[here, after:] = sh[:, 0:up]
                    ul[here, after:] = sl[:, 0:up]
                    th, tl = split_bf16(scaled[:, 0:up].T)
                    lh[after:, here] = th
                    ll[after:, here] = tl
                if kk:
                    mh[here, 0 : kk * BLK] = sh[:, up : HALF - BLK]
                    ml[here, 0 : kk * BLK] = sl[:, up : HALF - BLK]
                mh[here, here] = ih
                ml[here, here] = il
                zh[here, :] = sh[:, HALF - BLK :]
                zl[here, :] = sl[:, HALF - BLK :]

        return 0

    lax.fori_loop(0, blocks, step, 0)


def first_kernel(
    place_ref, own_ref, other_ref, out_ref, mh_out, ml_out, rest_out, cross_out,
    lh, ll, uh, ul, zh, zl, de, row, sym_ref, mh_ref, ml_ref, rest_ref, cross_ref, sem
):
    core = place_ref[0]
    for q in range(16):
        at = pl.multiple_of(q * STRIP + core * 32, 32)
        sym_ref[pl.ds(at, 32), :] = own_ref[q]
        at = pl.multiple_of(q * STRIP + (1 - core) * 32, 32)
        sym_ref[pl.ds(at, 32), :] = other_ref[q]
    blocks = NB // BLK
    for i in range(blocks):
        for j in range(i, blocks):
            a = sym_ref[i * BLK : (i + 1) * BLK, j * BLK : (j + 1) * BLK]
            b = sym_ref[j * BLK : (j + 1) * BLK, i * BLK : (i + 1) * BLK]
            s = (a + b.T) * 0.5
            sym_ref[i * BLK : (i + 1) * BLK, j * BLK : (j + 1) * BLK] = s
            if j > i:
                sym_ref[j * BLK : (j + 1) * BLK, i * BLK : (i + 1) * BLK] = s.T
    moves = [pltpu.make_async_copy(sym_ref, out_ref, sem.at[0])]
    moves[0].start()
    factor_half(
        sym_ref.at[0:HALF, 0:HALF], sym_ref.at[0:HALF, HALF:], lh, ll, uh, ul, mh_ref, ml_ref, zh, zl, de, row
    )
    for n, (x, y) in enumerate([(mh_ref, mh_out), (ml_ref, ml_out)]):
        moves.append(pltpu.make_async_copy(x, y, sem.at[1 + n]))
        moves[-1].start()
    th = zh[...].astype(jnp.float32).T.astype(jnp.bfloat16)
    tl = zl[...].astype(jnp.float32).T.astype(jnp.bfloat16)
    rest_ref[...] = sym_ref[HALF:, HALF:] - dot3(th, tl, zh[...], zl[...])
    moves.append(pltpu.make_async_copy(rest_ref, rest_out, sem.at[3]))
    moves[-1].start()
    cross_ref[...] = -dot3(th, tl, mh_ref[...], ml_ref[...])
    moves.append(pltpu.make_async_copy(cross_ref, cross_out, sem.at[4]))
    moves[-1].start()
    for move in moves:
        move.wait()


def second_kernel(
    place_ref, rest_in, cross_in, mh_in, ml_in, c_in, d_in, wt_ref,
    lh, ll, uh, ul, nh, nl, zh, zl, de, row, rest_ref, cross_ref, mh_ref, ml_ref, c_ref, d_ref, c_all, sem
):
    strip = place_ref[1]
    pairs = [(rest_in, rest_ref), (cross_in, cross_ref), (mh_in, mh_ref), (ml_in, ml_ref), (c_in, c_ref), (d_in, d_ref)]
    moves = [pltpu.make_async_copy(x, y, sem.at[n]) for n, (x, y) in enumerate(pairs)]
    for move in moves:
        move.start()
    for move in moves[:2]:
        move.wait()
    factor_half(rest_ref, cross_ref, lh, ll, uh, ul, nh, nl, zh, zl, de, row)
    for move in moves[2:]:
        move.wait()

    def joined(x, y):
        return x.astype(jnp.float32) + y.astype(jnp.float32)

    for s in range(2):

        @pl.when(strip == s)
        def _(s=s):
            at = slice(256 * s, 256 * s + 256)
            wt_ref[:, 0:HALF] = -joined(mh_ref[at, :], ml_ref[at, :])
            wt_ref[:, HALF:] = jnp.zeros((256, HALF), jnp.float32)

        @pl.when(strip == s + 2)
        def _(s=s):
            at = slice(256 * s, 256 * s + 256)
            wt_ref[:, 0:HALF] = -joined(zh[at, :], zl[at, :])
            wt_ref[:, HALF:] = -joined(nh[at, :], nl[at, :])

    @pl.when(strip >= 4)
    def _():
        core = place_ref[0]
        for q in range(16):
            at = pl.multiple_of(q * STRIP + core * RUN, RUN)
            c_all[pl.ds(at, RUN), :] = c_ref[q]
            at = pl.multiple_of(q * STRIP + (1 - core) * RUN, RUN)
            c_all[pl.ds(at, RUN), :] = d_ref[q]
        ch, cl = split_bf16(c_all[0:HALF, :])
        dh, dl = split_bf16(c_all[HALF:, :])
        low = dot3(zh[...], zl[...], ch, cl) + dot3(nh[...], nl[...], dh, dl)
        th, tl = split_bf16(low.T)
        high = dot3(mh_ref[...], ml_ref[...], ch, cl)
        sh, sl = split_bf16(high.T)
        wt_ref[:, 0:HALF] = dot3(sh, sl, mh_ref[...], ml_ref[...]) + dot3(th, tl, zh[...], zl[...])
        wt_ref[:, HALF:] = dot3(th, tl, nh[...], nl[...])


SQUARE = (HALF, HALF)


def factor_scratch(count):
    return [pltpu.VMEM(SQUARE, jnp.bfloat16)] * count + [
        pltpu.VMEM((BLK, 2 * BLK), jnp.float32),
        pltpu.VMEM((BLK, NB), jnp.float32),
    ]


def first_half(place, own, other):
    vmem = pl.BlockSpec(memory_space=pltpu.VMEM)
    hbm = pl.BlockSpec(memory_space=pltpu.HBM)
    shapes = [((NB, NB), jnp.float32)] + [(SQUARE, jnp.bfloat16)] * 2 + [(SQUARE, jnp.float32)] * 2
    return pl.pallas_call(
        first_kernel,
        in_specs=[pl.BlockSpec(memory_space=pltpu.SMEM), vmem, vmem],
        out_specs=[hbm] * 5,
        out_shape=[jax.ShapeDtypeStruct(*shape) for shape in shapes],
        scratch_shapes=factor_scratch(6) + [pltpu.VMEM(*shape) for shape in shapes] + [pltpu.SemaphoreType.DMA((5,))],
        compiler_params=pltpu.CompilerParams(vmem_limit_bytes=60 * 1024 * 1024),
        cost_estimate=pl.CostEstimate(flops=30_000_000_000, bytes_accessed=12 << 20, transcendentals=0),
        name="first_half",
    )(place, own, other)


def second_half(place, rest, cross, mh, ml, c_turned, d_turned):
    hbm = pl.BlockSpec(memory_space=pltpu.HBM)
    arrays = (rest, cross, mh, ml, c_turned, d_turned)
    return pl.pallas_call(
        second_kernel,
        in_specs=[pl.BlockSpec(memory_space=pltpu.SMEM)] + [hbm] * 6,
        out_specs=pl.BlockSpec(memory_space=pltpu.VMEM),
        out_shape=jax.ShapeDtypeStruct((256, NB), jnp.float32),
        scratch_shapes=factor_scratch(8)
        + [pltpu.VMEM(x.shape, x.dtype) for x in arrays]
        + [pltpu.VMEM((NB, 256), jnp.float32), pltpu.SemaphoreType.DMA((6,))],
        compiler_params=pltpu.CompilerParams(vmem_limit_bytes=60 * 1024 * 1024),
        cost_estimate=pl.CostEstimate(flops=1_000_000_000, bytes_accessed=6 << 20, transcendentals=0),
        name="second_half",
    )(place, *arrays)


def product_kernel(inv_ref, flags_ref, wt_ref, rows_ref, sym_ref, front_ref, child_ref, out_ref, wh, wl):
    t = pl.program_id(0)

    @pl.when(t == 0)
    def _():
        high, low = split_bf16(wt_ref[...])
        wh[...] = high
        wl[...] = low

    use_sym = jnp.logical_and(flags_ref[0] == 1, t < NB // TILE)
    a = jnp.where(use_sym, sym_ref[...], rows_ref[...])
    ah, al = split_bf16(a)
    term = dot3(wh[...], wl[...], ah, al).T
    keep = flags_ref[1] == 0
    for b in range(TILE // BLK):
        part = front_ref[0, b * BLK : (b + 1) * BLK, :]
        for s in range(2):
            n = inv_ref[s, (TILE // BLK) * t + b]
            part = part + jnp.where(n >= 0, child_ref[jnp.maximum(n, 0) * 2 + s], 0.0)
        part = jnp.where(keep, part, 0.0)
        out_ref[b * BLK : (b + 1) * BLK, :] = part - term[b * BLK : (b + 1) * BLK, :]


def product(inv, flags, wt, rows, sym, front, child):
    def sym_tile(t, flags):
        return jnp.where(flags[0] == 1, jnp.minimum(t, NB // TILE - 1), 0)

    return pl.pallas_call(
        product_kernel,
        grid_spec=pltpu.PrefetchScalarGridSpec(
            num_scalar_prefetch=2,
            grid=(2048 // TILE,),
            in_specs=[
                pl.BlockSpec((256, NB), lambda t, i, f: (0, 0)),
                pl.BlockSpec((NB, TILE), lambda t, i, f: (0, t)),
                pl.BlockSpec((NB, TILE), lambda t, i, f: (0, sym_tile(t, f))),
                pl.BlockSpec((1, TILE, 256), lambda t, i, f: (t, 0, 0)),
                pl.BlockSpec((16, BLK, 256), lambda t, i, f: (0, 0, 0)),
            ],
            out_specs=pl.BlockSpec((TILE, 256), lambda t, i, f: (t, 0)),
            scratch_shapes=[pltpu.VMEM((256, NB), jnp.bfloat16), pltpu.VMEM((256, NB), jnp.bfloat16)],
        ),
        out_shape=jax.ShapeDtypeStruct((2048, 256), jnp.float32),
        compiler_params=pltpu.CompilerParams(vmem_limit_bytes=60 * 1024 * 1024),
        cost_estimate=pl.CostEstimate(flops=3 * 2 * 2048 * 1024 * 256, bytes_accessed=16 << 20, transcendentals=0),
        name="product",
    )(inv, flags, wt, rows, sym, front, child)


def body(child_update, parent_front, row_map, col_map):
    half = lax.axis_index("half")
    row = lax.axis_index("row")
    col = lax.axis_index("col")
    strip = half * 8 + col
    targets = jnp.arange(W // BLK, dtype=jnp.int32)
    own_columns = lax.dynamic_index_in_dim(col_map, half, 0, keepdims=False)
    match = (own_columns[:, None] == targets[None, :]).astype(jnp.int32)
    source = jnp.sum(match * jnp.arange(8, dtype=jnp.int32)[:, None], 0)
    hit = jnp.sum(match, 0)
    rows = jnp.concatenate([row_map[:, 0] - row * 16, jnp.where(half == 0, 1, 0)[None]]).astype(jnp.int32)
    strips, wide = prep(child_update[0], parent_front, source, hit, rows)

    pieces = lax.all_to_all(strips, PLANE, 0, 0, tiled=True)
    where = pieces[1::2, 0, BLK : 3 * BLK : BLK].T.astype(jnp.int32)
    core = row % 2
    chip = (row // 2)[None]
    place = jnp.stack([core, strip]).astype(jnp.int32)
    swap = [(i, i ^ 1) for i in range(16)]
    a_strip, keep, give = assemble_strip(pieces, where, place)

    start, wanted = share(place, keep, lax.ppermute(give, "row", swap))
    halves = [lax.ppermute(start, "row", [(0, 2 * z), (1, 2 * z + 1)]) for z in range(1, 8)]
    spread = pick(chip, [start] + halves, copies=16)

    matching = lax.all_to_all(wanted, PLANE, 0, 0, tiled=True)
    child = lax.all_to_all(wide, PLANE, 0, 0, tiled=True)
    late_strip, spread = lax.optimization_barrier((a_strip, spread))
    a_turned = lax.all_gather(late_strip, PLANE, axis=0, tiled=True)
    spread, matching, child = lax.optimization_barrier((spread, matching, child))
    gathered = lax.all_to_all(spread, PLANE, 0, 0, tiled=True)
    other = lax.ppermute(gathered, "row", swap)
    parent_then, _ = lax.optimization_barrier((parent_front, spread))
    turned_parent = turn(parent_then)

    def along(x, pairs):
        return lax.ppermute(x, "row", [(2 * i + n, 2 * j + n) for i, j in pairs for n in range(2)])

    mine = jnp.where(row < 2, matching, 0.0)
    to_3, to_6 = along(matching, [(0, 3)]), along(matching, [(0, 6)])
    to_3, to_6, turned_parent = lax.optimization_barrier((to_3, to_6, turned_parent))
    relay = mine + (to_3 + to_6)
    gathered, relay, turned_parent = lax.optimization_barrier((gathered, relay, turned_parent))
    front = lax.all_to_all(turned_parent, "col", 0, 0, tiled=True)
    last = [along(relay, [(0, 1), (3, 4), (6, 7)]), along(relay, [(3, 2), (6, 5)])]
    sym, mh, ml, rest, cross = first_half(place, gathered, other)

    rest, relay, *last = lax.optimization_barrier((rest, relay, *last))
    c_turned = relay + (last[0] + last[1])
    d_turned = lax.ppermute(c_turned, "row", swap)
    wt = second_half(place, rest, cross, mh, ml, c_turned, d_turned)

    blocks = jnp.arange(16, dtype=jnp.int32)
    order = jnp.arange(8, dtype=jnp.int32)
    inv = jnp.max(jnp.where(where[:, :, None] == blocks[None, None, :], order[None, :, None], -1), axis=1)
    flags = jnp.stack([(row == 0).astype(jnp.int32), (strip < 4).astype(jnp.int32)])
    return product(inv, flags, wt, a_turned, sym, front, child)


def solution(mesh):
    return jax.shard_map(
        body,
        mesh=mesh,
        in_specs=(
            P("half", ("row", "col"), None),
            P(("row", "col"), "half"),
            P(None, ("row", "col")),
            P(),
        ),
        out_specs=P("row", ("half", "col")),
        check_vma=False,
    )
```

```python
import jax
import jax.numpy as jnp
from jax import lax
from jax.experimental import pallas as pl
from jax.experimental.pallas import tpu as pltpu
from jax.sharding import PartitionSpec as P

BLK = 128
NB = 1024
W = 4096
STRIP = 64
RUN = 32
HALF = NB // 2
TILE = 256
PLANE = ("col", "half")
VMEM_LIMIT = 24 * 1024 * 1024


def prep_kernel(src_ref, hit_ref, child_ref, parent_ref, rows_ref, strips_ref, wide_ref):
    is_first_half = rows_ref[2]
    for w in range(W // BLK):
        start = pl.multiple_of(src_ref[w] * BLK, BLK)
        block = jnp.where(hit_ref[w] > 0, child_ref[:, pl.ds(start, BLK)], 0.0)
        j = w // 2
        q = (j % 8) * 2 + j // 8
        wide_ref[q, :, (w % 2) * BLK : (w % 2 + 1) * BLK] = block
        if w < NB // BLK:
            turned = block.T
            strips_ref[2 * w, :, 0:BLK] = turned[0:STRIP]
            strips_ref[2 * w + 1, :, 0:BLK] = turned[STRIP:BLK]

    @pl.when(is_first_half == 1)
    def _():
        for w in range(NB // BLK):
            turned = parent_ref[:, w * BLK : (w + 1) * BLK].T
            strips_ref[2 * w, :, BLK : 3 * BLK] = turned[0:STRIP]
            strips_ref[2 * w + 1, :, BLK : 3 * BLK] = turned[STRIP:BLK]

    @pl.when(is_first_half != 1)
    def _():
        for s in range(2):
            value = jnp.full((STRIP, BLK), rows_ref[s], jnp.int32).astype(jnp.float32)
            for d in range(16):
                strips_ref[d, :, (1 + s) * BLK : (2 + s) * BLK] = value


def prep(child, parent, source, hit, rows):
    smem = pl.BlockSpec(memory_space=pltpu.SMEM)
    return pl.pallas_call(
        prep_kernel,
        grid=(1,),
        in_specs=[
            smem,
            smem,
            pl.BlockSpec((BLK, NB), lambda i: (0, 0)),
            pl.BlockSpec((2 * BLK, NB), lambda i: (0, 0)),
            smem,
        ],
        out_specs=[
            pl.BlockSpec((16, STRIP, 3 * BLK), lambda i: (0, 0, 0)),
            pl.BlockSpec((16, BLK, 2 * BLK), lambda i: (0, 0, 0)),
        ],
        out_shape=[
            jax.ShapeDtypeStruct((16, STRIP, 3 * BLK), jnp.float32),
            jax.ShapeDtypeStruct((16, BLK, 2 * BLK), jnp.float32),
        ],
        compiler_params=pltpu.CompilerParams(vmem_limit_bytes=VMEM_LIMIT),
        name="prep",
    )(source, hit, child, parent, rows)


def strip_kernel(where_ref, place_ref, pieces_ref, out_ref, keep_ref, give_ref):
    core = place_ref[0]
    for c in range(8):
        out_ref[:, 256 * c : 256 * (c + 1)] = pieces_ref[2 * c, :, BLK : 3 * BLK]
    for c in range(8):
        for s in range(2):
            at = pl.multiple_of(where_ref[s, c] * BLK, BLK)
            out_ref[:, pl.ds(at, BLK)] += pieces_ref[2 * c + s, :, 0:BLK]
    keep_ref[...] = out_ref[pl.ds(pl.multiple_of(core * RUN, RUN), RUN), :]
    give_ref[...] = out_ref[pl.ds(pl.multiple_of((1 - core) * RUN, RUN), RUN), :]


def assemble_strip(pieces, where, place):
    smem = pl.BlockSpec(memory_space=pltpu.SMEM)
    vmem = pl.BlockSpec(memory_space=pltpu.VMEM)
    half = jax.ShapeDtypeStruct((RUN, 2048), jnp.float32)
    return pl.pallas_call(
        strip_kernel,
        in_specs=[smem, smem, vmem],
        out_specs=[vmem] * 3,
        out_shape=[jax.ShapeDtypeStruct((STRIP, 2048), jnp.float32), half, half],
        compiler_params=pltpu.CompilerParams(vmem_limit_bytes=24 * 1024 * 1024),
        name="strip",
    )(where, place, pieces)


def share_kernel(place_ref, keep_ref, got_ref, start_ref, wanted_ref):
    core = place_ref[0]
    start_ref[...] = jnp.where(core == 0, keep_ref[:, 0:NB], got_ref[:, 0:NB])
    for c in range(8):
        a = keep_ref[:, 256 * c : 256 * (c + 1)]
        b = got_ref[:, 256 * c : 256 * (c + 1)]
        wanted_ref[2 * c] = jnp.where(core == 0, a, b)
        wanted_ref[2 * c + 1] = jnp.where(core == 0, b, a)


def share(place, keep, got):
    vmem = pl.BlockSpec(memory_space=pltpu.VMEM)
    return pl.pallas_call(
        share_kernel,
        in_specs=[pl.BlockSpec(memory_space=pltpu.SMEM), vmem, vmem],
        out_specs=[vmem] * 2,
        out_shape=[
            jax.ShapeDtypeStruct((RUN, NB), jnp.float32),
            jax.ShapeDtypeStruct((16, RUN, 256), jnp.float32),
        ],
        compiler_params=pltpu.CompilerParams(vmem_limit_bytes=16 * 1024 * 1024),
        name="share",
    )(place, keep, got)


def turn_kernel(parent_ref, out_ref):
    for n in range(8):
        out_ref[n] = parent_ref[:, 256 * n : 256 * (n + 1)]


def turn(parent):
    vmem = pl.BlockSpec(memory_space=pltpu.VMEM)
    return pl.pallas_call(
        turn_kernel,
        in_specs=[vmem],
        out_specs=vmem,
        out_shape=jax.ShapeDtypeStruct((8, 256, 256), jnp.float32),
        compiler_params=pltpu.CompilerParams(vmem_limit_bytes=16 * 1024 * 1024),
        cost_estimate=pl.CostEstimate(flops=60_000_000_000, bytes_accessed=4 << 20, transcendentals=0),
        name="turn",
    )(parent)


def pick_kernel(copies, index_ref, *refs):
    out_ref = refs[-1]
    for i in range(len(refs) - 1):

        @pl.when(index_ref[0] == i)
        def _(i=i):
            if copies:
                for n in range(copies):
                    out_ref[n] = refs[i][...]
            else:
                out_ref[...] = refs[i][...]


def pick(index, arrays, copies=0):
    shape = arrays[0].shape
    vmem = pl.BlockSpec(memory_space=pltpu.VMEM)
    return pl.pallas_call(
        lambda *refs: pick_kernel(copies, *refs),
        in_specs=[pl.BlockSpec(memory_space=pltpu.SMEM)] + [vmem] * len(arrays),
        out_specs=vmem,
        out_shape=jax.ShapeDtypeStruct((copies,) + shape if copies else shape, arrays[0].dtype),
        compiler_params=pltpu.CompilerParams(vmem_limit_bytes=16 * 1024 * 1024),
        name="pick",
    )(index, *arrays)


def split_bf16(x):
    high = x.astype(jnp.bfloat16)
    return high, (x - high.astype(jnp.float32)).astype(jnp.bfloat16)


def dot3(xh, xl, yh, yl):
    def dot(x, y):
        return lax.dot_general(x, y, (((1,), (0,)), ((), ())), preferred_element_type=jnp.float32)

    return dot(xh, yh) + (dot(xh, yl) + dot(xl, yh))


def lane(x, i):
    return jnp.broadcast_to(x[:, i : i + 1], (8, BLK))


def sub(x, i):
    return jnp.broadcast_to(x[i : i + 1, :], (8, x.shape[1]))


def eliminate(d, e, base):
    groups = len(d)
    place = lax.broadcasted_iota(jnp.int32, (8, BLK), 0)
    for g in range(groups):
        first = base + 8 * g
        columns = [lane(d[g], first + i) for i in range(8)]
        below = [[lane(d[n], first + i) for i in range(8)] for n in range(g + 1, groups)]
        scales = jnp.zeros((8, BLK), jnp.float32)
        for i in range(8):
            r = lax.rsqrt(sub(columns[i], i))
            scales = jnp.where(place == i, r, scales)
            l = columns[i] * r
            low = [b[i] * r for b in below]
            for m in range(i + 1, 8):
                f = sub(l, m)
                columns[m] = columns[m] - l * f
                for n, b in enumerate(below):
                    b[m] = b[m] - low[n] * f
            dr = sub(d[g], i) * r
            er = sub(e[g], i) * r
            masked = jnp.where(place > i, l, 0.0)
            d[g] = d[g] - masked * dr
            e[g] = e[g] - masked * er
            for n in range(len(below)):
                d[g + 1 + n] = d[g + 1 + n] - low[n] * dr
                e[g + 1 + n] = e[g + 1 + n] - low[n] * er
        d[g] = d[g] * scales
        e[g] = e[g] * scales
    return d, e


GROUP = 32


def factor_block(de_ref):
    for p in range(BLK // GROUP):
        base = p * GROUP
        rows = [slice(base + 8 * g, base + 8 * g + 8) for g in range(GROUP // 8)]
        d = [de_ref[r, 0:BLK] for r in rows]
        e = [de_ref[r, BLK : 2 * BLK] for r in rows]
        d, e = eliminate(d, e, base)
        for r, x, y in zip(rows, d, e):
            de_ref[r, 0:BLK] = x
            de_ref[r, BLK : 2 * BLK] = y
        if base + GROUP < BLK:
            done = de_ref[base : base + GROUP, :]
            left = done[:, 0:BLK].T[base + GROUP :]
            lh, ll = split_bf16(left)
            rh, rl = split_bf16(done)
            de_ref[base + GROUP :, :] -= dot3(lh, ll, rh, rl)


def factor_half(a_ref, r_ref, lh, ll, uh, ul, mh, ml, zh, zl, de, row):
    blocks = HALF // BLK
    mh[...] = jnp.zeros_like(mh)
    ml[...] = jnp.zeros_like(ml)
    eye = (
        lax.broadcasted_iota(jnp.int32, (BLK, BLK), 0) == lax.broadcasted_iota(jnp.int32, (BLK, BLK), 1)
    ).astype(jnp.float32)

    def step(k, _):
        for kk in range(blocks):

            @pl.when(k == kk)
            def _(kk=kk):
                here = slice(kk * BLK, (kk + 1) * BLK)
                done = kk * BLK
                up = HALF - done
                if kk == 0:
                    row[:, 0:HALF] = a_ref[here, 0:HALF]
                    row[:, HALF:] = r_ref[here, :]
                else:
                    x, y = lh[here, 0:done], ll[here, 0:done]
                    row[:, 0:up] = a_ref[here, done:HALF] - dot3(x, y, uh[0:done, done:], ul[0:done, done:])
                    row[:, up:HALF] = -dot3(x, y, mh[0:done, 0:done], ml[0:done, 0:done])
                    row[:, HALF:] = r_ref[here, :] - dot3(x, y, zh[0:done, :], zl[0:done, :])

        de[:, 0:BLK] = row[:, 0:BLK]
        de[:, BLK:] = eye
        factor_block(de)
        ih, il = split_bf16(de[:, BLK:])
        rh, rl = split_bf16(row[:, BLK:])
        scaled = dot3(ih, il, rh, rl)
        sh, sl = split_bf16(scaled)
        for kk in range(blocks):

            @pl.when(k == kk)
            def _(kk=kk):
                here = slice(kk * BLK, (kk + 1) * BLK)
                after = (kk + 1) * BLK
                up = HALF - after
                if up:
                    uh[here, after:] = sh[:, 0:up]
                    ul[here, after:] = sl[:, 0:up]
                    th, tl = split_bf16(scaled[:, 0:up].T)
                    lh[after:, here] = th
                    ll[after:, here] = tl
                if kk:
                    mh[here, 0 : kk * BLK] = sh[:, up : HALF - BLK]
                    ml[here, 0 : kk * BLK] = sl[:, up : HALF - BLK]
                mh[here, here] = ih
                ml[here, here] = il
                zh[here, :] = sh[:, HALF - BLK :]
                zl[here, :] = sl[:, HALF - BLK :]

        return 0

    lax.fori_loop(0, blocks, step, 0)


def first_kernel(
    place_ref, own_ref, other_ref, out_ref, mh_out, ml_out, rest_out, cross_out,
    lh, ll, uh, ul, zh, zl, de, row, sym_ref, mh_ref, ml_ref, rest_ref, cross_ref, sem
):
    core = place_ref[0]
    for q in range(16):
        at = pl.multiple_of(q * STRIP + core * 32, 32)
        sym_ref[pl.ds(at, 32), :] = own_ref[q]
        at = pl.multiple_of(q * STRIP + (1 - core) * 32, 32)
        sym_ref[pl.ds(at, 32), :] = other_ref[q]
    blocks = NB // BLK
    for i in range(blocks):
        for j in range(i, blocks):
            a = sym_ref[i * BLK : (i + 1) * BLK, j * BLK : (j + 1) * BLK]
            b = sym_ref[j * BLK : (j + 1) * BLK, i * BLK : (i + 1) * BLK]
            s = (a + b.T) * 0.5
            sym_ref[i * BLK : (i + 1) * BLK, j * BLK : (j + 1) * BLK] = s
            if j > i:
                sym_ref[j * BLK : (j + 1) * BLK, i * BLK : (i + 1) * BLK] = s.T
    moves = [pltpu.make_async_copy(sym_ref, out_ref, sem.at[0])]
    moves[0].start()
    factor_half(
        sym_ref.at[0:HALF, 0:HALF], sym_ref.at[0:HALF, HALF:], lh, ll, uh, ul, mh_ref, ml_ref, zh, zl, de, row
    )
    for n, (x, y) in enumerate([(mh_ref, mh_out), (ml_ref, ml_out)]):
        moves.append(pltpu.make_async_copy(x, y, sem.at[1 + n]))
        moves[-1].start()
    th = zh[...].astype(jnp.float32).T.astype(jnp.bfloat16)
    tl = zl[...].astype(jnp.float32).T.astype(jnp.bfloat16)
    rest_ref[...] = sym_ref[HALF:, HALF:] - dot3(th, tl, zh[...], zl[...])
    moves.append(pltpu.make_async_copy(rest_ref, rest_out, sem.at[3]))
    moves[-1].start()
    cross_ref[...] = -dot3(th, tl, mh_ref[...], ml_ref[...])
    moves.append(pltpu.make_async_copy(cross_ref, cross_out, sem.at[4]))
    moves[-1].start()
    for move in moves:
        move.wait()


def second_kernel(
    place_ref, rest_in, cross_in, mh_in, ml_in, c_in, d_in, wt_ref,
    lh, ll, uh, ul, nh, nl, zh, zl, de, row, rest_ref, cross_ref, mh_ref, ml_ref, c_ref, d_ref, c_all, sem
):
    strip = place_ref[1]
    pairs = [(rest_in, rest_ref), (cross_in, cross_ref), (mh_in, mh_ref), (ml_in, ml_ref), (c_in, c_ref), (d_in, d_ref)]
    moves = [pltpu.make_async_copy(x, y, sem.at[n]) for n, (x, y) in enumerate(pairs)]
    for move in moves:
        move.start()
    for move in moves[:2]:
        move.wait()
    factor_half(rest_ref, cross_ref, lh, ll, uh, ul, nh, nl, zh, zl, de, row)
    for move in moves[2:]:
        move.wait()

    def joined(x, y):
        return x.astype(jnp.float32) + y.astype(jnp.float32)

    for s in range(2):

        @pl.when(strip == s)
        def _(s=s):
            at = slice(256 * s, 256 * s + 256)
            wt_ref[:, 0:HALF] = -joined(mh_ref[at, :], ml_ref[at, :])
            wt_ref[:, HALF:] = jnp.zeros((256, HALF), jnp.float32)

        @pl.when(strip == s + 2)
        def _(s=s):
            at = slice(256 * s, 256 * s + 256)
            wt_ref[:, 0:HALF] = -joined(zh[at, :], zl[at, :])
            wt_ref[:, HALF:] = -joined(nh[at, :], nl[at, :])

    @pl.when(strip >= 4)
    def _():
        core = place_ref[0]
        for q in range(16):
            at = pl.multiple_of(q * STRIP + core * RUN, RUN)
            c_all[pl.ds(at, RUN), :] = c_ref[q]
            at = pl.multiple_of(q * STRIP + (1 - core) * RUN, RUN)
            c_all[pl.ds(at, RUN), :] = d_ref[q]
        ch, cl = split_bf16(c_all[0:HALF, :])
        dh, dl = split_bf16(c_all[HALF:, :])
        low = dot3(zh[...], zl[...], ch, cl) + dot3(nh[...], nl[...], dh, dl)
        th, tl = split_bf16(low.T)
        high = dot3(mh_ref[...], ml_ref[...], ch, cl)
        sh, sl = split_bf16(high.T)
        wt_ref[:, 0:HALF] = dot3(sh, sl, mh_ref[...], ml_ref[...]) + dot3(th, tl, zh[...], zl[...])
        wt_ref[:, HALF:] = dot3(th, tl, nh[...], nl[...])


SQUARE = (HALF, HALF)


def factor_scratch(count):
    return [pltpu.VMEM(SQUARE, jnp.bfloat16)] * count + [
        pltpu.VMEM((BLK, 2 * BLK), jnp.float32),
        pltpu.VMEM((BLK, NB), jnp.float32),
    ]


def first_half(place, own, other):
    vmem = pl.BlockSpec(memory_space=pltpu.VMEM)
    hbm = pl.BlockSpec(memory_space=pltpu.HBM)
    shapes = [((NB, NB), jnp.float32)] + [(SQUARE, jnp.bfloat16)] * 2 + [(SQUARE, jnp.float32)] * 2
    return pl.pallas_call(
        first_kernel,
        in_specs=[pl.BlockSpec(memory_space=pltpu.SMEM), vmem, vmem],
        out_specs=[hbm] * 5,
        out_shape=[jax.ShapeDtypeStruct(*shape) for shape in shapes],
        scratch_shapes=factor_scratch(6) + [pltpu.VMEM(*shape) for shape in shapes] + [pltpu.SemaphoreType.DMA((5,))],
        compiler_params=pltpu.CompilerParams(vmem_limit_bytes=60 * 1024 * 1024),
        cost_estimate=pl.CostEstimate(flops=30_000_000_000, bytes_accessed=12 << 20, transcendentals=0),
        name="first_half",
    )(place, own, other)


def second_half(place, rest, cross, mh, ml, c_turned, d_turned):
    hbm = pl.BlockSpec(memory_space=pltpu.HBM)
    arrays = (rest, cross, mh, ml, c_turned, d_turned)
    return pl.pallas_call(
        second_kernel,
        in_specs=[pl.BlockSpec(memory_space=pltpu.SMEM)] + [hbm] * 6,
        out_specs=pl.BlockSpec(memory_space=pltpu.VMEM),
        out_shape=jax.ShapeDtypeStruct((256, NB), jnp.float32),
        scratch_shapes=factor_scratch(8)
        + [pltpu.VMEM(x.shape, x.dtype) for x in arrays]
        + [pltpu.VMEM((NB, 256), jnp.float32), pltpu.SemaphoreType.DMA((6,))],
        compiler_params=pltpu.CompilerParams(vmem_limit_bytes=60 * 1024 * 1024),
        cost_estimate=pl.CostEstimate(flops=30_000_000_000, bytes_accessed=6 << 20, transcendentals=0),
        name="second_half",
    )(place, *arrays)


def product_kernel(inv_ref, flags_ref, wt_ref, rows_ref, sym_ref, front_ref, child_ref, out_ref, wh, wl):
    t = pl.program_id(0)

    @pl.when(t == 0)
    def _():
        high, low = split_bf16(wt_ref[...])
        wh[...] = high
        wl[...] = low

    use_sym = jnp.logical_and(flags_ref[0] == 1, t < NB // TILE)
    a = jnp.where(use_sym, sym_ref[...], rows_ref[...])
    ah, al = split_bf16(a)
    term = dot3(wh[...], wl[...], ah, al).T
    keep = flags_ref[1] == 0
    for b in range(TILE // BLK):
        part = front_ref[0, b * BLK : (b + 1) * BLK, :]
        for s in range(2):
            n = inv_ref[s, (TILE // BLK) * t + b]
            part = part + jnp.where(n >= 0, child_ref[jnp.maximum(n, 0) * 2 + s], 0.0)
        part = jnp.where(keep, part, 0.0)
        out_ref[b * BLK : (b + 1) * BLK, :] = part - term[b * BLK : (b + 1) * BLK, :]


def product(inv, flags, wt, rows, sym, front, child):
    def sym_tile(t, flags):
        return jnp.where(flags[0] == 1, jnp.minimum(t, NB // TILE - 1), 0)

    return pl.pallas_call(
        product_kernel,
        grid_spec=pltpu.PrefetchScalarGridSpec(
            num_scalar_prefetch=2,
            grid=(2048 // TILE,),
            in_specs=[
                pl.BlockSpec((256, NB), lambda t, i, f: (0, 0)),
                pl.BlockSpec((NB, TILE), lambda t, i, f: (0, t)),
                pl.BlockSpec((NB, TILE), lambda t, i, f: (0, sym_tile(t, f))),
                pl.BlockSpec((1, TILE, 256), lambda t, i, f: (t, 0, 0)),
                pl.BlockSpec((16, BLK, 256), lambda t, i, f: (0, 0, 0)),
            ],
            out_specs=pl.BlockSpec((TILE, 256), lambda t, i, f: (t, 0)),
            scratch_shapes=[pltpu.VMEM((256, NB), jnp.bfloat16), pltpu.VMEM((256, NB), jnp.bfloat16)],
        ),
        out_shape=jax.ShapeDtypeStruct((2048, 256), jnp.float32),
        compiler_params=pltpu.CompilerParams(vmem_limit_bytes=60 * 1024 * 1024),
        cost_estimate=pl.CostEstimate(flops=3 * 2 * 2048 * 1024 * 256, bytes_accessed=16 << 20, transcendentals=0),
        name="product",
    )(inv, flags, wt, rows, sym, front, child)


def body(child_update, parent_front, row_map, col_map):
    half = lax.axis_index("half")
    row = lax.axis_index("row")
    col = lax.axis_index("col")
    strip = half * 8 + col
    targets = jnp.arange(W // BLK, dtype=jnp.int32)
    own_columns = lax.dynamic_index_in_dim(col_map, half, 0, keepdims=False)
    match = (own_columns[:, None] == targets[None, :]).astype(jnp.int32)
    source = jnp.sum(match * jnp.arange(8, dtype=jnp.int32)[:, None], 0)
    hit = jnp.sum(match, 0)
    rows = jnp.concatenate([row_map[:, 0] - row * 16, jnp.where(half == 0, 1, 0)[None]]).astype(jnp.int32)
    strips, wide = prep(child_update[0], parent_front, source, hit, rows)

    pieces = lax.all_to_all(strips, PLANE, 0, 0, tiled=True)
    where = pieces[1::2, 0, BLK : 3 * BLK : BLK].T.astype(jnp.int32)
    core = row % 2
    chip = (row // 2)[None]
    place = jnp.stack([core, strip]).astype(jnp.int32)
    swap = [(i, i ^ 1) for i in range(16)]
    a_strip, keep, give = assemble_strip(pieces, where, place)

    start, wanted = share(place, keep, lax.ppermute(give, "row", swap))
    halves = [lax.ppermute(start, "row", [(0, 2 * z), (1, 2 * z + 1)]) for z in range(1, 8)]
    spread = pick(chip, [start] + halves, copies=16)

    matching = lax.all_to_all(wanted, PLANE, 0, 0, tiled=True)
    child = lax.all_to_all(wide, PLANE, 0, 0, tiled=True)
    late_strip, spread = lax.optimization_barrier((a_strip, spread))
    a_turned = lax.all_gather(late_strip, PLANE, axis=0, tiled=True)
    spread, matching, child = lax.optimization_barrier((spread, matching, child))
    gathered = lax.all_to_all(spread, PLANE, 0, 0, tiled=True)
    other = lax.ppermute(gathered, "row", swap)
    parent_then, _ = lax.optimization_barrier((parent_front, spread))
    turned_parent = turn(parent_then)

    def along(x, pairs):
        return lax.ppermute(x, "row", [(2 * i + n, 2 * j + n) for i, j in pairs for n in range(2)])

    mine = jnp.where(row < 2, matching, 0.0)
    to_3, to_6 = along(matching, [(0, 3)]), along(matching, [(0, 6)])
    to_3, to_6, turned_parent = lax.optimization_barrier((to_3, to_6, turned_parent))
    relay = mine + (to_3 + to_6)
    gathered, relay, turned_parent = lax.optimization_barrier((gathered, relay, turned_parent))
    front = lax.all_to_all(turned_parent, "col", 0, 0, tiled=True)
    last = [along(relay, [(0, 1), (3, 4), (6, 7)]), along(relay, [(3, 2), (6, 5)])]
    sym, mh, ml, rest, cross = first_half(place, gathered, other)

    rest, relay, *last = lax.optimization_barrier((rest, relay, *last))
    c_turned = relay + (last[0] + last[1])
    d_turned = lax.ppermute(c_turned, "row", swap)
    wt = second_half(place, rest, cross, mh, ml, c_turned, d_turned)

    blocks = jnp.arange(16, dtype=jnp.int32)
    order = jnp.arange(8, dtype=jnp.int32)
    inv = jnp.max(jnp.where(where[:, :, None] == blocks[None, None, :], order[None, :, None], -1), axis=1)
    flags = jnp.stack([(row == 0).astype(jnp.int32), (strip < 4).astype(jnp.int32)])
    return product(inv, flags, wt, a_turned, sym, front, child)


def solution(mesh):
    return jax.shard_map(
        body,
        mesh=mesh,
        in_specs=(
            P("half", ("row", "col"), None),
            P(("row", "col"), "half"),
            P(None, ("row", "col")),
            P(),
        ),
        out_specs=P("row", ("half", "col")),
        check_vma=False,
    )
```

```python
import jax
import jax.numpy as jnp
from jax import lax
from jax.experimental import pallas as pl
from jax.experimental.pallas import tpu as pltpu
from jax.sharding import PartitionSpec as P

BLK = 128
NB = 1024
W = 4096
STRIP = 64
RUN = 32
HALF = NB // 2
TILE = 512
PLANE = ("col", "half")
VMEM_LIMIT = 24 * 1024 * 1024


def prep_kernel(src_ref, hit_ref, child_ref, parent_ref, rows_ref, strips_ref, wide_ref):
    is_first_half = rows_ref[2]
    for w in range(W // BLK):
        start = pl.multiple_of(src_ref[w] * BLK, BLK)
        block = jnp.where(hit_ref[w] > 0, child_ref[:, pl.ds(start, BLK)], 0.0)
        j = w // 2
        q = (j % 8) * 2 + j // 8
        wide_ref[q, :, (w % 2) * BLK : (w % 2 + 1) * BLK] = block
        if w < NB // BLK:
            turned = block.T
            strips_ref[2 * w, :, 0:BLK] = turned[0:STRIP]
            strips_ref[2 * w + 1, :, 0:BLK] = turned[STRIP:BLK]

    @pl.when(is_first_half == 1)
    def _():
        for w in range(NB // BLK):
            turned = parent_ref[:, w * BLK : (w + 1) * BLK].T
            strips_ref[2 * w, :, BLK : 3 * BLK] = turned[0:STRIP]
            strips_ref[2 * w + 1, :, BLK : 3 * BLK] = turned[STRIP:BLK]

    @pl.when(is_first_half != 1)
    def _():
        for s in range(2):
            value = jnp.full((STRIP, BLK), rows_ref[s], jnp.int32).astype(jnp.float32)
            for d in range(16):
                strips_ref[d, :, (1 + s) * BLK : (2 + s) * BLK] = value


def prep(child, parent, source, hit, rows):
    smem = pl.BlockSpec(memory_space=pltpu.SMEM)
    return pl.pallas_call(
        prep_kernel,
        grid=(1,),
        in_specs=[
            smem,
            smem,
            pl.BlockSpec((BLK, NB), lambda i: (0, 0)),
            pl.BlockSpec((2 * BLK, NB), lambda i: (0, 0)),
            smem,
        ],
        out_specs=[
            pl.BlockSpec((16, STRIP, 3 * BLK), lambda i: (0, 0, 0)),
            pl.BlockSpec((16, BLK, 2 * BLK), lambda i: (0, 0, 0)),
        ],
        out_shape=[
            jax.ShapeDtypeStruct((16, STRIP, 3 * BLK), jnp.float32),
            jax.ShapeDtypeStruct((16, BLK, 2 * BLK), jnp.float32),
        ],
        compiler_params=pltpu.CompilerParams(vmem_limit_bytes=VMEM_LIMIT),
        name="prep",
    )(source, hit, child, parent, rows)


def strip_kernel(where_ref, place_ref, pieces_ref, out_ref, keep_ref, give_ref):
    core = place_ref[0]
    for c in range(8):
        out_ref[:, 256 * c : 256 * (c + 1)] = pieces_ref[2 * c, :, BLK : 3 * BLK]
    for c in range(8):
        for s in range(2):
            at = pl.multiple_of(where_ref[s, c] * BLK, BLK)
            out_ref[:, pl.ds(at, BLK)] += pieces_ref[2 * c + s, :, 0:BLK]
    keep_ref[...] = out_ref[pl.ds(pl.multiple_of(core * RUN, RUN), RUN), :]
    give_ref[...] = out_ref[pl.ds(pl.multiple_of((1 - core) * RUN, RUN), RUN), :]


def assemble_strip(pieces, where, place):
    smem = pl.BlockSpec(memory_space=pltpu.SMEM)
    vmem = pl.BlockSpec(memory_space=pltpu.VMEM)
    half = jax.ShapeDtypeStruct((RUN, 2048), jnp.float32)
    return pl.pallas_call(
        strip_kernel,
        in_specs=[smem, smem, vmem],
        out_specs=[vmem] * 3,
        out_shape=[jax.ShapeDtypeStruct((STRIP, 2048), jnp.float32), half, half],
        compiler_params=pltpu.CompilerParams(vmem_limit_bytes=24 * 1024 * 1024),
        name="strip",
    )(where, place, pieces)


def share_kernel(place_ref, keep_ref, got_ref, start_ref, wanted_ref):
    core = place_ref[0]
    start_ref[...] = jnp.where(core == 0, keep_ref[:, 0:NB], got_ref[:, 0:NB])
    for c in range(8):
        a = keep_ref[:, 256 * c : 256 * (c + 1)]
        b = got_ref[:, 256 * c : 256 * (c + 1)]
        wanted_ref[2 * c] = jnp.where(core == 0, a, b)
        wanted_ref[2 * c + 1] = jnp.where(core == 0, b, a)


def share(place, keep, got):
    vmem = pl.BlockSpec(memory_space=pltpu.VMEM)
    return pl.pallas_call(
        share_kernel,
        in_specs=[pl.BlockSpec(memory_space=pltpu.SMEM), vmem, vmem],
        out_specs=[vmem] * 2,
        out_shape=[
            jax.ShapeDtypeStruct((RUN, NB), jnp.float32),
            jax.ShapeDtypeStruct((16, RUN, 256), jnp.float32),
        ],
        compiler_params=pltpu.CompilerParams(vmem_limit_bytes=16 * 1024 * 1024),
        name="share",
    )(place, keep, got)


def turn_kernel(parent_ref, out_ref):
    for n in range(8):
        out_ref[n] = parent_ref[:, 256 * n : 256 * (n + 1)]


def turn(parent):
    vmem = pl.BlockSpec(memory_space=pltpu.VMEM)
    return pl.pallas_call(
        turn_kernel,
        in_specs=[vmem],
        out_specs=vmem,
        out_shape=jax.ShapeDtypeStruct((8, 256, 256), jnp.float32),
        compiler_params=pltpu.CompilerParams(vmem_limit_bytes=16 * 1024 * 1024),
        cost_estimate=pl.CostEstimate(flops=60_000_000_000, bytes_accessed=4 << 20, transcendentals=0),
        name="turn",
    )(parent)


def pick_kernel(copies, index_ref, *refs):
    out_ref = refs[-1]
    for i in range(len(refs) - 1):

        @pl.when(index_ref[0] == i)
        def _(i=i):
            if copies:
                for n in range(copies):
                    out_ref[n] = refs[i][...]
            else:
                out_ref[...] = refs[i][...]


def pick(index, arrays, copies=0):
    shape = arrays[0].shape
    vmem = pl.BlockSpec(memory_space=pltpu.VMEM)
    return pl.pallas_call(
        lambda *refs: pick_kernel(copies, *refs),
        in_specs=[pl.BlockSpec(memory_space=pltpu.SMEM)] + [vmem] * len(arrays),
        out_specs=vmem,
        out_shape=jax.ShapeDtypeStruct((copies,) + shape if copies else shape, arrays[0].dtype),
        compiler_params=pltpu.CompilerParams(vmem_limit_bytes=16 * 1024 * 1024),
        name="pick",
    )(index, *arrays)


def split_bf16(x):
    high = x.astype(jnp.bfloat16)
    return high, (x - high.astype(jnp.float32)).astype(jnp.bfloat16)


def dot3(xh, xl, yh, yl):
    def dot(x, y):
        return lax.dot_general(x, y, (((1,), (0,)), ((), ())), preferred_element_type=jnp.float32)

    return dot(xh, yh) + (dot(xh, yl) + dot(xl, yh))


def lane(x, i):
    return jnp.broadcast_to(x[:, i : i + 1], (8, BLK))


def sub(x, i):
    return jnp.broadcast_to(x[i : i + 1, :], (8, x.shape[1]))


def eliminate(d, e, base):
    groups = len(d)
    place = lax.broadcasted_iota(jnp.int32, (8, BLK), 0)
    for g in range(groups):
        first = base + 8 * g
        columns = [lane(d[g], first + i) for i in range(8)]
        below = [[lane(d[n], first + i) for i in range(8)] for n in range(g + 1, groups)]
        scales = jnp.zeros((8, BLK), jnp.float32)
        for i in range(8):
            r = lax.rsqrt(sub(columns[i], i))
            scales = jnp.where(place == i, r, scales)
            l = columns[i] * r
            low = [b[i] * r for b in below]
            for m in range(i + 1, 8):
                f = sub(l, m)
                columns[m] = columns[m] - l * f
                for n, b in enumerate(below):
                    b[m] = b[m] - low[n] * f
            dr = sub(d[g], i) * r
            er = sub(e[g], i) * r
            masked = jnp.where(place > i, l, 0.0)
            d[g] = d[g] - masked * dr
            e[g] = e[g] - masked * er
            for n in range(len(below)):
                d[g + 1 + n] = d[g + 1 + n] - low[n] * dr
                e[g + 1 + n] = e[g + 1 + n] - low[n] * er
        d[g] = d[g] * scales
        e[g] = e[g] * scales
    return d, e


GROUP = 32


def factor_block(de_ref):
    for p in range(BLK // GROUP):
        base = p * GROUP
        rows = [slice(base + 8 * g, base + 8 * g + 8) for g in range(GROUP // 8)]
        d = [de_ref[r, 0:BLK] for r in rows]
        e = [de_ref[r, BLK : 2 * BLK] for r in rows]
        d, e = eliminate(d, e, base)
        for r, x, y in zip(rows, d, e):
            de_ref[r, 0:BLK] = x
            de_ref[r, BLK : 2 * BLK] = y
        if base + GROUP < BLK:
            done = de_ref[base : base + GROUP, :]
            left = done[:, 0:BLK].T[base + GROUP :]
            lh, ll = split_bf16(left)
            rh, rl = split_bf16(done)
            de_ref[base + GROUP :, :] -= dot3(lh, ll, rh, rl)


def factor_half(a_ref, r_ref, lh, ll, uh, ul, mh, ml, zh, zl, de, row):
    blocks = HALF // BLK
    mh[...] = jnp.zeros_like(mh)
    ml[...] = jnp.zeros_like(ml)
    eye = (
        lax.broadcasted_iota(jnp.int32, (BLK, BLK), 0) == lax.broadcasted_iota(jnp.int32, (BLK, BLK), 1)
    ).astype(jnp.float32)

    def step(k, _):
        for kk in range(blocks):

            @pl.when(k == kk)
            def _(kk=kk):
                here = slice(kk * BLK, (kk + 1) * BLK)
                done = kk * BLK
                up = HALF - done
                if kk == 0:
                    row[:, 0:HALF] = a_ref[here, 0:HALF]
                    row[:, HALF:] = r_ref[here, :]
                else:
                    x, y = lh[here, 0:done], ll[here, 0:done]
                    row[:, 0:up] = a_ref[here, done:HALF] - dot3(x, y, uh[0:done, done:], ul[0:done, done:])
                    row[:, up:HALF] = -dot3(x, y, mh[0:done, 0:done], ml[0:done, 0:done])
                    row[:, HALF:] = r_ref[here, :] - dot3(x, y, zh[0:done, :], zl[0:done, :])

        de[:, 0:BLK] = row[:, 0:BLK]
        de[:, BLK:] = eye
        factor_block(de)
        ih, il = split_bf16(de[:, BLK:])
        rh, rl = split_bf16(row[:, BLK:])
        scaled = dot3(ih, il, rh, rl)
        sh, sl = split_bf16(scaled)
        for kk in range(blocks):

            @pl.when(k == kk)
            def _(kk=kk):
                here = slice(kk * BLK, (kk + 1) * BLK)
                after = (kk + 1) * BLK
                up = HALF - after
                if up:
                    uh[here, after:] = sh[:, 0:up]
                    ul[here, after:] = sl[:, 0:up]
                    th, tl = split_bf16(scaled[:, 0:up].T)
                    lh[after:, here] = th
                    ll[after:, here] = tl
                if kk:
                    mh[here, 0 : kk * BLK] = sh[:, up : HALF - BLK]
                    ml[here, 0 : kk * BLK] = sl[:, up : HALF - BLK]
                mh[here, here] = ih
                ml[here, here] = il
                zh[here, :] = sh[:, HALF - BLK :]
                zl[here, :] = sl[:, HALF - BLK :]

        return 0

    lax.fori_loop(0, blocks, step, 0)


def first_kernel(
    place_ref, own_ref, other_ref, out_ref, mh_out, ml_out, rest_out, cross_out,
    lh, ll, uh, ul, zh, zl, de, row, sym_ref, mh_ref, ml_ref, rest_ref, cross_ref, sem
):
    core = place_ref[0]
    for q in range(16):
        at = pl.multiple_of(q * STRIP + core * 32, 32)
        sym_ref[pl.ds(at, 32), :] = own_ref[q]
        at = pl.multiple_of(q * STRIP + (1 - core) * 32, 32)
        sym_ref[pl.ds(at, 32), :] = other_ref[q]
    blocks = NB // BLK
    for i in range(blocks):
        for j in range(i, blocks):
            a = sym_ref[i * BLK : (i + 1) * BLK, j * BLK : (j + 1) * BLK]
            b = sym_ref[j * BLK : (j + 1) * BLK, i * BLK : (i + 1) * BLK]
            s = (a + b.T) * 0.5
            sym_ref[i * BLK : (i + 1) * BLK, j * BLK : (j + 1) * BLK] = s
            if j > i:
                sym_ref[j * BLK : (j + 1) * BLK, i * BLK : (i + 1) * BLK] = s.T
    moves = [pltpu.make_async_copy(sym_ref, out_ref, sem.at[0])]
    moves[0].start()
    factor_half(
        sym_ref.at[0:HALF, 0:HALF], sym_ref.at[0:HALF, HALF:], lh, ll, uh, ul, mh_ref, ml_ref, zh, zl, de, row
    )
    for n, (x, y) in enumerate([(mh_ref, mh_out), (ml_ref, ml_out)]):
        moves.append(pltpu.make_async_copy(x, y, sem.at[1 + n]))
        moves[-1].start()
    th = zh[...].astype(jnp.float32).T.astype(jnp.bfloat16)
    tl = zl[...].astype(jnp.float32).T.astype(jnp.bfloat16)
    rest_ref[...] = sym_ref[HALF:, HALF:] - dot3(th, tl, zh[...], zl[...])
    moves.append(pltpu.make_async_copy(rest_ref, rest_out, sem.at[3]))
    moves[-1].start()
    cross_ref[...] = -dot3(th, tl, mh_ref[...], ml_ref[...])
    moves.append(pltpu.make_async_copy(cross_ref, cross_out, sem.at[4]))
    moves[-1].start()
    for move in moves:
        move.wait()


def second_kernel(
    place_ref, rest_in, cross_in, mh_in, ml_in, c_in, d_in, wt_ref,
    lh, ll, uh, ul, nh, nl, zh, zl, de, row, rest_ref, cross_ref, mh_ref, ml_ref, c_ref, d_ref, c_all, sem
):
    strip = place_ref[1]
    pairs = [(rest_in, rest_ref), (cross_in, cross_ref), (mh_in, mh_ref), (ml_in, ml_ref), (c_in, c_ref), (d_in, d_ref)]
    moves = [pltpu.make_async_copy(x, y, sem.at[n]) for n, (x, y) in enumerate(pairs)]
    for move in moves:
        move.start()
    for move in moves[:2]:
        move.wait()
    factor_half(rest_ref, cross_ref, lh, ll, uh, ul, nh, nl, zh, zl, de, row)
    for move in moves[2:]:
        move.wait()

    def joined(x, y):
        return x.astype(jnp.float32) + y.astype(jnp.float32)

    for s in range(2):

        @pl.when(strip == s)
        def _(s=s):
            at = slice(256 * s, 256 * s + 256)
            wt_ref[:, 0:HALF] = -joined(mh_ref[at, :], ml_ref[at, :])
            wt_ref[:, HALF:] = jnp.zeros((256, HALF), jnp.float32)

        @pl.when(strip == s + 2)
        def _(s=s):
            at = slice(256 * s, 256 * s + 256)
            wt_ref[:, 0:HALF] = -joined(zh[at, :], zl[at, :])
            wt_ref[:, HALF:] = -joined(nh[at, :], nl[at, :])

    @pl.when(strip >= 4)
    def _():
        core = place_ref[0]
        for q in range(16):
            at = pl.multiple_of(q * STRIP + core * RUN, RUN)
            c_all[pl.ds(at, RUN), :] = c_ref[q]
            at = pl.multiple_of(q * STRIP + (1 - core) * RUN, RUN)
            c_all[pl.ds(at, RUN), :] = d_ref[q]
        ch, cl = split_bf16(c_all[0:HALF, :])
        dh, dl = split_bf16(c_all[HALF:, :])
        low = dot3(zh[...], zl[...], ch, cl) + dot3(nh[...], nl[...], dh, dl)
        th, tl = split_bf16(low.T)
        high = dot3(mh_ref[...], ml_ref[...], ch, cl)
        sh, sl = split_bf16(high.T)
        wt_ref[:, 0:HALF] = dot3(sh, sl, mh_ref[...], ml_ref[...]) + dot3(th, tl, zh[...], zl[...])
        wt_ref[:, HALF:] = dot3(th, tl, nh[...], nl[...])


SQUARE = (HALF, HALF)


def factor_scratch(count):
    return [pltpu.VMEM(SQUARE, jnp.bfloat16)] * count + [
        pltpu.VMEM((BLK, 2 * BLK), jnp.float32),
        pltpu.VMEM((BLK, NB), jnp.float32),
    ]


def first_half(place, own, other):
    vmem = pl.BlockSpec(memory_space=pltpu.VMEM)
    hbm = pl.BlockSpec(memory_space=pltpu.HBM)
    shapes = [((NB, NB), jnp.float32)] + [(SQUARE, jnp.bfloat16)] * 2 + [(SQUARE, jnp.float32)] * 2
    return pl.pallas_call(
        first_kernel,
        in_specs=[pl.BlockSpec(memory_space=pltpu.SMEM), vmem, vmem],
        out_specs=[hbm] * 5,
        out_shape=[jax.ShapeDtypeStruct(*shape) for shape in shapes],
        scratch_shapes=factor_scratch(6) + [pltpu.VMEM(*shape) for shape in shapes] + [pltpu.SemaphoreType.DMA((5,))],
        compiler_params=pltpu.CompilerParams(vmem_limit_bytes=60 * 1024 * 1024),
        cost_estimate=pl.CostEstimate(flops=30_000_000_000, bytes_accessed=12 << 20, transcendentals=0),
        name="first_half",
    )(place, own, other)


def second_half(place, rest, cross, mh, ml, c_turned, d_turned):
    hbm = pl.BlockSpec(memory_space=pltpu.HBM)
    arrays = (rest, cross, mh, ml, c_turned, d_turned)
    return pl.pallas_call(
        second_kernel,
        in_specs=[pl.BlockSpec(memory_space=pltpu.SMEM)] + [hbm] * 6,
        out_specs=pl.BlockSpec(memory_space=pltpu.VMEM),
        out_shape=jax.ShapeDtypeStruct((256, NB), jnp.float32),
        scratch_shapes=factor_scratch(8)
        + [pltpu.VMEM(x.shape, x.dtype) for x in arrays]
        + [pltpu.VMEM((NB, 256), jnp.float32), pltpu.SemaphoreType.DMA((6,))],
        compiler_params=pltpu.CompilerParams(vmem_limit_bytes=60 * 1024 * 1024),
        cost_estimate=pl.CostEstimate(flops=1_000_000_000, bytes_accessed=6 << 20, transcendentals=0),
        name="second_half",
    )(place, *arrays)


def product_kernel(inv_ref, flags_ref, wt_ref, rows_ref, sym_ref, front_ref, child_ref, out_ref, wh, wl):
    t = pl.program_id(0)

    @pl.when(t == 0)
    def _():
        high, low = split_bf16(wt_ref[...])
        wh[...] = high
        wl[...] = low

    use_sym = jnp.logical_and(flags_ref[0] == 1, t < NB // TILE)
    a = jnp.where(use_sym, sym_ref[...], rows_ref[...])
    ah, al = split_bf16(a)
    term = dot3(wh[...], wl[...], ah, al).T
    keep = flags_ref[1] == 0
    for b in range(TILE // BLK):
        part = front_ref[b // 2, (b % 2) * BLK : (b % 2 + 1) * BLK, :]
        for s in range(2):
            n = inv_ref[s, (TILE // BLK) * t + b]
            part = part + jnp.where(n >= 0, child_ref[jnp.maximum(n, 0) * 2 + s], 0.0)
        part = jnp.where(keep, part, 0.0)
        out_ref[b * BLK : (b + 1) * BLK, :] = part - term[b * BLK : (b + 1) * BLK, :]


def product(inv, flags, wt, rows, sym, front, child):
    def sym_tile(t, flags):
        return jnp.where(flags[0] == 1, jnp.minimum(t, NB // TILE - 1), 0)

    return pl.pallas_call(
        product_kernel,
        grid_spec=pltpu.PrefetchScalarGridSpec(
            num_scalar_prefetch=2,
            grid=(2048 // TILE,),
            in_specs=[
                pl.BlockSpec((256, NB), lambda t, i, f: (0, 0)),
                pl.BlockSpec((NB, TILE), lambda t, i, f: (0, t)),
                pl.BlockSpec((NB, TILE), lambda t, i, f: (0, sym_tile(t, f))),
                pl.BlockSpec((TILE // 256, 256, 256), lambda t, i, f: (t, 0, 0)),
                pl.BlockSpec((16, BLK, 256), lambda t, i, f: (0, 0, 0)),
            ],
            out_specs=pl.BlockSpec((TILE, 256), lambda t, i, f: (t, 0)),
            scratch_shapes=[pltpu.VMEM((256, NB), jnp.bfloat16), pltpu.VMEM((256, NB), jnp.bfloat16)],
        ),
        out_shape=jax.ShapeDtypeStruct((2048, 256), jnp.float32),
        compiler_params=pltpu.CompilerParams(vmem_limit_bytes=60 * 1024 * 1024),
        cost_estimate=pl.CostEstimate(flops=3 * 2 * 2048 * 1024 * 256, bytes_accessed=16 << 20, transcendentals=0),
        name="product",
    )(inv, flags, wt, rows, sym, front, child)


def body(child_update, parent_front, row_map, col_map):
    half = lax.axis_index("half")
    row = lax.axis_index("row")
    col = lax.axis_index("col")
    strip = half * 8 + col
    targets = jnp.arange(W // BLK, dtype=jnp.int32)
    own_columns = lax.dynamic_index_in_dim(col_map, half, 0, keepdims=False)
    match = (own_columns[:, None] == targets[None, :]).astype(jnp.int32)
    source = jnp.sum(match * jnp.arange(8, dtype=jnp.int32)[:, None], 0)
    hit = jnp.sum(match, 0)
    rows = jnp.concatenate([row_map[:, 0] - row * 16, jnp.where(half == 0, 1, 0)[None]]).astype(jnp.int32)
    strips, wide = prep(child_update[0], parent_front, source, hit, rows)

    pieces = lax.all_to_all(strips, PLANE, 0, 0, tiled=True)
    where = pieces[1::2, 0, BLK : 3 * BLK : BLK].T.astype(jnp.int32)
    core = row % 2
    chip = (row // 2)[None]
    place = jnp.stack([core, strip]).astype(jnp.int32)
    swap = [(i, i ^ 1) for i in range(16)]
    a_strip, keep, give = assemble_strip(pieces, where, place)

    start, wanted = share(place, keep, lax.ppermute(give, "row", swap))
    halves = [lax.ppermute(start, "row", [(0, 2 * z), (1, 2 * z + 1)]) for z in range(1, 8)]
    child = lax.all_to_all(wide, PLANE, 0, 0, tiled=True)
    start, child, *halves = lax.optimization_barrier((start, child, *halves))
    spread = pick(chip, [start] + halves, copies=16)

    matching = lax.all_to_all(wanted, PLANE, 0, 0, tiled=True)
    late_strip, spread = lax.optimization_barrier((a_strip, spread))
    a_turned = lax.all_gather(late_strip, PLANE, axis=0, tiled=True)
    spread, matching = lax.optimization_barrier((spread, matching))
    gathered = lax.all_to_all(spread, PLANE, 0, 0, tiled=True)
    parent_then, _ = lax.optimization_barrier((parent_front, spread))
    turned_parent = turn(parent_then)

    def along(x, pairs):
        return lax.ppermute(x, "row", [(2 * i + n, 2 * j + n) for i, j in pairs for n in range(2)])

    mine = jnp.where(row < 2, matching, 0.0)
    to_3, to_6 = along(matching, [(0, 3)]), along(matching, [(0, 6)])
    to_3, to_6, turned_parent = lax.optimization_barrier((to_3, to_6, turned_parent))
    relay = mine + (to_3 + to_6)
    gathered, relay, turned_parent = lax.optimization_barrier((gathered, relay, turned_parent))
    other = lax.ppermute(gathered, "row", swap)
    front = lax.all_to_all(turned_parent, "col", 0, 0, tiled=True)
    last = [along(relay, [(0, 1), (3, 4), (6, 7)]), along(relay, [(3, 2), (6, 5)])]
    sym, mh, ml, rest, cross = first_half(place, gathered, other)

    rest, relay, *last = lax.optimization_barrier((rest, relay, *last))
    c_turned = relay + (last[0] + last[1])
    d_turned = lax.ppermute(c_turned, "row", swap)
    wt = second_half(place, rest, cross, mh, ml, c_turned, d_turned)

    blocks = jnp.arange(16, dtype=jnp.int32)
    order = jnp.arange(8, dtype=jnp.int32)
    inv = jnp.max(jnp.where(where[:, :, None] == blocks[None, None, :], order[None, :, None], -1), axis=1)
    flags = jnp.stack([(row == 0).astype(jnp.int32), (strip < 4).astype(jnp.int32)])
    return product(inv, flags, wt, a_turned, sym, front, child)


def solution(mesh):
    return jax.shard_map(
        body,
        mesh=mesh,
        in_specs=(
            P("half", ("row", "col"), None),
            P(("row", "col"), "half"),
            P(None, ("row", "col")),
            P(),
        ),
        out_specs=P("row", ("half", "col")),
        check_vma=False,
    )
```

```python
import jax
import jax.numpy as jnp
from jax import lax
from jax.experimental import pallas as pl
from jax.experimental.pallas import tpu as pltpu
from jax.sharding import PartitionSpec as P

BLK = 128
NB = 1024
W = 4096
STRIP = 64
RUN = 32
HALF = NB // 2
TILE = 512
PLANE = ("col", "half")
VMEM_LIMIT = 24 * 1024 * 1024


def prep_kernel(src_ref, hit_ref, child_ref, parent_ref, rows_ref, strips_ref, wide_ref):
    is_first_half = rows_ref[2]
    for w in range(W // BLK):
        start = pl.multiple_of(src_ref[w] * BLK, BLK)
        block = jnp.where(hit_ref[w] > 0, child_ref[:, pl.ds(start, BLK)], 0.0)
        j = w // 2
        q = (j % 8) * 2 + j // 8
        wide_ref[q, :, (w % 2) * BLK : (w % 2 + 1) * BLK] = block
        if w < NB // BLK:
            turned = block.T
            strips_ref[2 * w, :, 0:BLK] = turned[0:STRIP]
            strips_ref[2 * w + 1, :, 0:BLK] = turned[STRIP:BLK]

    @pl.when(is_first_half == 1)
    def _():
        for w in range(NB // BLK):
            turned = parent_ref[:, w * BLK : (w + 1) * BLK].T
            strips_ref[2 * w, :, BLK : 3 * BLK] = turned[0:STRIP]
            strips_ref[2 * w + 1, :, BLK : 3 * BLK] = turned[STRIP:BLK]

    @pl.when(is_first_half != 1)
    def _():
        for s in range(2):
            value = jnp.full((STRIP, BLK), rows_ref[s], jnp.int32).astype(jnp.float32)
            for d in range(16):
                strips_ref[d, :, (1 + s) * BLK : (2 + s) * BLK] = value


def prep(child, parent, source, hit, rows):
    smem = pl.BlockSpec(memory_space=pltpu.SMEM)
    return pl.pallas_call(
        prep_kernel,
        grid=(1,),
        in_specs=[
            smem,
            smem,
            pl.BlockSpec((BLK, NB), lambda i: (0, 0)),
            pl.BlockSpec((2 * BLK, NB), lambda i: (0, 0)),
            smem,
        ],
        out_specs=[
            pl.BlockSpec((16, STRIP, 3 * BLK), lambda i: (0, 0, 0)),
            pl.BlockSpec((16, BLK, 2 * BLK), lambda i: (0, 0, 0)),
        ],
        out_shape=[
            jax.ShapeDtypeStruct((16, STRIP, 3 * BLK), jnp.float32),
            jax.ShapeDtypeStruct((16, BLK, 2 * BLK), jnp.float32),
        ],
        compiler_params=pltpu.CompilerParams(vmem_limit_bytes=VMEM_LIMIT),
        name="prep",
    )(source, hit, child, parent, rows)


def strip_kernel(where_ref, place_ref, pieces_ref, out_ref, keep_ref, give_ref):
    core = place_ref[0]
    for c in range(8):
        out_ref[:, 256 * c : 256 * (c + 1)] = pieces_ref[2 * c, :, BLK : 3 * BLK]
    for c in range(8):
        for s in range(2):
            at = pl.multiple_of(where_ref[s, c] * BLK, BLK)
            out_ref[:, pl.ds(at, BLK)] += pieces_ref[2 * c + s, :, 0:BLK]
    keep_ref[...] = out_ref[pl.ds(pl.multiple_of(core * RUN, RUN), RUN), :]
    give_ref[...] = out_ref[pl.ds(pl.multiple_of((1 - core) * RUN, RUN), RUN), :]


def assemble_strip(pieces, where, place):
    smem = pl.BlockSpec(memory_space=pltpu.SMEM)
    vmem = pl.BlockSpec(memory_space=pltpu.VMEM)
    half = jax.ShapeDtypeStruct((RUN, 2048), jnp.float32)
    return pl.pallas_call(
        strip_kernel,
        in_specs=[smem, smem, vmem],
        out_specs=[vmem] * 3,
        out_shape=[jax.ShapeDtypeStruct((STRIP, 2048), jnp.float32), half, half],
        compiler_params=pltpu.CompilerParams(vmem_limit_bytes=24 * 1024 * 1024),
        name="strip",
    )(where, place, pieces)


def share_kernel(place_ref, keep_ref, got_ref, start_ref, wanted_ref):
    core = place_ref[0]
    start_ref[...] = jnp.where(core == 0, keep_ref[:, 0:NB], got_ref[:, 0:NB])
    for c in range(8):
        a = keep_ref[:, 256 * c : 256 * (c + 1)]
        b = got_ref[:, 256 * c : 256 * (c + 1)]
        wanted_ref[2 * c] = jnp.where(core == 0, a, b)
        wanted_ref[2 * c + 1] = jnp.where(core == 0, b, a)


def share(place, keep, got):
    vmem = pl.BlockSpec(memory_space=pltpu.VMEM)
    return pl.pallas_call(
        share_kernel,
        in_specs=[pl.BlockSpec(memory_space=pltpu.SMEM), vmem, vmem],
        out_specs=[vmem] * 2,
        out_shape=[
            jax.ShapeDtypeStruct((RUN, NB), jnp.float32),
            jax.ShapeDtypeStruct((16, RUN, 256), jnp.float32),
        ],
        compiler_params=pltpu.CompilerParams(vmem_limit_bytes=16 * 1024 * 1024),
        name="share",
    )(place, keep, got)


def turn_kernel(parent_ref, out_ref):
    for n in range(8):
        out_ref[n] = parent_ref[:, 256 * n : 256 * (n + 1)]


def turn(parent):
    vmem = pl.BlockSpec(memory_space=pltpu.VMEM)
    return pl.pallas_call(
        turn_kernel,
        in_specs=[vmem],
        out_specs=vmem,
        out_shape=jax.ShapeDtypeStruct((8, 256, 256), jnp.float32),
        compiler_params=pltpu.CompilerParams(vmem_limit_bytes=16 * 1024 * 1024),
        cost_estimate=pl.CostEstimate(flops=60_000_000_000, bytes_accessed=4 << 20, transcendentals=0),
        name="turn",
    )(parent)


def pick_kernel(copies, index_ref, *refs):
    out_ref = refs[-1]
    for i in range(len(refs) - 1):

        @pl.when(index_ref[0] == i)
        def _(i=i):
            if copies:
                for n in range(copies):
                    out_ref[n] = refs[i][...]
            else:
                out_ref[...] = refs[i][...]


def pick(index, arrays, copies=0):
    shape = arrays[0].shape
    vmem = pl.BlockSpec(memory_space=pltpu.VMEM)
    return pl.pallas_call(
        lambda *refs: pick_kernel(copies, *refs),
        in_specs=[pl.BlockSpec(memory_space=pltpu.SMEM)] + [vmem] * len(arrays),
        out_specs=vmem,
        out_shape=jax.ShapeDtypeStruct((copies,) + shape if copies else shape, arrays[0].dtype),
        compiler_params=pltpu.CompilerParams(vmem_limit_bytes=16 * 1024 * 1024),
        name="pick",
    )(index, *arrays)


def split_bf16(x):
    high = x.astype(jnp.bfloat16)
    return high, (x - high.astype(jnp.float32)).astype(jnp.bfloat16)


def dot3(xh, xl, yh, yl):
    def dot(x, y):
        return lax.dot_general(x, y, (((1,), (0,)), ((), ())), preferred_element_type=jnp.float32)

    return dot(xh, yh) + (dot(xh, yl) + dot(xl, yh))


def lane(x, i):
    return jnp.broadcast_to(x[:, i : i + 1], (8, BLK))


def sub(x, i):
    return jnp.broadcast_to(x[i : i + 1, :], (8, x.shape[1]))


def eliminate(d, e, base):
    groups = len(d)
    place = lax.broadcasted_iota(jnp.int32, (8, BLK), 0)
    for g in range(groups):
        first = base + 8 * g
        columns = [lane(d[g], first + i) for i in range(8)]
        below = [[lane(d[n], first + i) for i in range(8)] for n in range(g + 1, groups)]
        scales = jnp.zeros((8, BLK), jnp.float32)
        for i in range(8):
            r = lax.rsqrt(sub(columns[i], i))
            scales = jnp.where(place == i, r, scales)
            l = columns[i] * r
            low = [b[i] * r for b in below]
            for m in range(i + 1, 8):
                f = sub(l, m)
                columns[m] = columns[m] - l * f
                for n, b in enumerate(below):
                    b[m] = b[m] - low[n] * f
            dr = sub(d[g], i) * r
            er = sub(e[g], i) * r
            masked = jnp.where(place > i, l, 0.0)
            d[g] = d[g] - masked * dr
            e[g] = e[g] - masked * er
            for n in range(len(below)):
                d[g + 1 + n] = d[g + 1 + n] - low[n] * dr
                e[g + 1 + n] = e[g + 1 + n] - low[n] * er
        d[g] = d[g] * scales
        e[g] = e[g] * scales
    return d, e


GROUP = 32


def factor_block(de_ref):
    for p in range(BLK // GROUP):
        base = p * GROUP
        rows = [slice(base + 8 * g, base + 8 * g + 8) for g in range(GROUP // 8)]
        d = [de_ref[r, 0:BLK] for r in rows]
        e = [de_ref[r, BLK : 2 * BLK] for r in rows]
        d, e = eliminate(d, e, base)
        for r, x, y in zip(rows, d, e):
            de_ref[r, 0:BLK] = x
            de_ref[r, BLK : 2 * BLK] = y
        if base + GROUP < BLK:
            done = de_ref[base : base + GROUP, :]
            left = done[:, 0:BLK].T[base + GROUP :]
            lh, ll = split_bf16(left)
            rh, rl = split_bf16(done)
            de_ref[base + GROUP :, :] -= dot3(lh, ll, rh, rl)


def factor_half(a_ref, r_ref, lh, ll, uh, ul, mh, ml, zh, zl, de, row):
    blocks = HALF // BLK
    mh[...] = jnp.zeros_like(mh)
    ml[...] = jnp.zeros_like(ml)
    eye = (
        lax.broadcasted_iota(jnp.int32, (BLK, BLK), 0) == lax.broadcasted_iota(jnp.int32, (BLK, BLK), 1)
    ).astype(jnp.float32)

    def step(k, _):
        for kk in range(blocks):

            @pl.when(k == kk)
            def _(kk=kk):
                here = slice(kk * BLK, (kk + 1) * BLK)
                done = kk * BLK
                up = HALF - done
                if kk == 0:
                    row[:, 0:HALF] = a_ref[here, 0:HALF]
                    row[:, HALF:] = r_ref[here, :]
                else:
                    x, y = lh[here, 0:done], ll[here, 0:done]
                    row[:, 0:up] = a_ref[here, done:HALF] - dot3(x, y, uh[0:done, done:], ul[0:done, done:])
                    row[:, up:HALF] = -dot3(x, y, mh[0:done, 0:done], ml[0:done, 0:done])
                    row[:, HALF:] = r_ref[here, :] - dot3(x, y, zh[0:done, :], zl[0:done, :])

        de[:, 0:BLK] = row[:, 0:BLK]
        de[:, BLK:] = eye
        factor_block(de)
        ih, il = split_bf16(de[:, BLK:])
        rh, rl = split_bf16(row[:, BLK:])
        scaled = dot3(ih, il, rh, rl)
        sh, sl = split_bf16(scaled)
        for kk in range(blocks):

            @pl.when(k == kk)
            def _(kk=kk):
                here = slice(kk * BLK, (kk + 1) * BLK)
                after = (kk + 1) * BLK
                up = HALF - after
                if up:
                    uh[here, after:] = sh[:, 0:up]
                    ul[here, after:] = sl[:, 0:up]
                    th, tl = split_bf16(scaled[:, 0:up].T)
                    lh[after:, here] = th
                    ll[after:, here] = tl
                if kk:
                    mh[here, 0 : kk * BLK] = sh[:, up : HALF - BLK]
                    ml[here, 0 : kk * BLK] = sl[:, up : HALF - BLK]
                mh[here, here] = ih
                ml[here, here] = il
                zh[here, :] = sh[:, HALF - BLK :]
                zl[here, :] = sl[:, HALF - BLK :]

        return 0

    lax.fori_loop(0, blocks, step, 0)


def first_kernel(
    place_ref, own_ref, other_ref, out_ref, mh_out, ml_out, rest_out, cross_out,
    lh, ll, uh, ul, zh, zl, de, row, sym_ref, mh_ref, ml_ref, rest_ref, cross_ref, sem
):
    core = place_ref[0]
    for q in range(16):
        at = pl.multiple_of(q * STRIP + core * 32, 32)
        sym_ref[pl.ds(at, 32), :] = own_ref[q]
        at = pl.multiple_of(q * STRIP + (1 - core) * 32, 32)
        sym_ref[pl.ds(at, 32), :] = other_ref[q]
    blocks = NB // BLK
    for i in range(blocks):
        for j in range(i, blocks):
            a = sym_ref[i * BLK : (i + 1) * BLK, j * BLK : (j + 1) * BLK]
            b = sym_ref[j * BLK : (j + 1) * BLK, i * BLK : (i + 1) * BLK]
            s = (a + b.T) * 0.5
            sym_ref[i * BLK : (i + 1) * BLK, j * BLK : (j + 1) * BLK] = s
            if j > i:
                sym_ref[j * BLK : (j + 1) * BLK, i * BLK : (i + 1) * BLK] = s.T
    moves = [pltpu.make_async_copy(sym_ref, out_ref, sem.at[0])]
    moves[0].start()
    factor_half(
        sym_ref.at[0:HALF, 0:HALF], sym_ref.at[0:HALF, HALF:], lh, ll, uh, ul, mh_ref, ml_ref, zh, zl, de, row
    )
    for n, (x, y) in enumerate([(mh_ref, mh_out), (ml_ref, ml_out)]):
        moves.append(pltpu.make_async_copy(x, y, sem.at[1 + n]))
        moves[-1].start()
    th = zh[...].astype(jnp.float32).T.astype(jnp.bfloat16)
    tl = zl[...].astype(jnp.float32).T.astype(jnp.bfloat16)
    rest_ref[...] = sym_ref[HALF:, HALF:] - dot3(th, tl, zh[...], zl[...])
    moves.append(pltpu.make_async_copy(rest_ref, rest_out, sem.at[3]))
    moves[-1].start()
    cross_ref[...] = -dot3(th, tl, mh_ref[...], ml_ref[...])
    moves.append(pltpu.make_async_copy(cross_ref, cross_out, sem.at[4]))
    moves[-1].start()
    for move in moves:
        move.wait()


def second_kernel(
    place_ref, rest_in, cross_in, mh_in, ml_in, c_in, d_in, wt_out,
    lh, ll, uh, ul, nh, nl, zh, zl, de, row, rest_ref, cross_ref, mh_ref, ml_ref, c_ref, d_ref, c_all, wt_ref, sem
):
    strip = place_ref[1]
    pairs = [(rest_in, rest_ref), (cross_in, cross_ref), (mh_in, mh_ref), (ml_in, ml_ref), (c_in, c_ref), (d_in, d_ref)]
    moves = [pltpu.make_async_copy(x, y, sem.at[n]) for n, (x, y) in enumerate(pairs)]
    for move in moves:
        move.start()
    for move in moves[:2]:
        move.wait()
    factor_half(rest_ref, cross_ref, lh, ll, uh, ul, nh, nl, zh, zl, de, row)
    for move in moves[2:]:
        move.wait()

    def joined(x, y):
        return x.astype(jnp.float32) + y.astype(jnp.float32)

    for s in range(2):

        @pl.when(strip == s)
        def _(s=s):
            at = slice(256 * s, 256 * s + 256)
            wt_ref[:, 0:HALF] = -joined(mh_ref[at, :], ml_ref[at, :])
            wt_ref[:, HALF:] = jnp.zeros((256, HALF), jnp.float32)

        @pl.when(strip == s + 2)
        def _(s=s):
            at = slice(256 * s, 256 * s + 256)
            wt_ref[:, 0:HALF] = -joined(zh[at, :], zl[at, :])
            wt_ref[:, HALF:] = -joined(nh[at, :], nl[at, :])

    @pl.when(strip >= 4)
    def _():
        core = place_ref[0]
        for q in range(16):
            at = pl.multiple_of(q * STRIP + core * RUN, RUN)
            c_all[pl.ds(at, RUN), :] = c_ref[q]
            at = pl.multiple_of(q * STRIP + (1 - core) * RUN, RUN)
            c_all[pl.ds(at, RUN), :] = d_ref[q]
        ch, cl = split_bf16(c_all[0:HALF, :])
        dh, dl = split_bf16(c_all[HALF:, :])
        low = dot3(zh[...], zl[...], ch, cl) + dot3(nh[...], nl[...], dh, dl)
        th, tl = split_bf16(low.T)
        high = dot3(mh_ref[...], ml_ref[...], ch, cl)
        sh, sl = split_bf16(high.T)
        wt_ref[:, 0:HALF] = dot3(sh, sl, mh_ref[...], ml_ref[...]) + dot3(th, tl, zh[...], zl[...])
        wt_ref[:, HALF:] = dot3(th, tl, nh[...], nl[...])

    move = pltpu.make_async_copy(wt_ref, wt_out, sem.at[6])
    move.start()
    move.wait()


SQUARE = (HALF, HALF)


def factor_scratch(count):
    return [pltpu.VMEM(SQUARE, jnp.bfloat16)] * count + [
        pltpu.VMEM((BLK, 2 * BLK), jnp.float32),
        pltpu.VMEM((BLK, NB), jnp.float32),
    ]


def first_half(place, own, other):
    vmem = pl.BlockSpec(memory_space=pltpu.VMEM)
    hbm = pl.BlockSpec(memory_space=pltpu.HBM)
    shapes = [((NB, NB), jnp.float32)] + [(SQUARE, jnp.bfloat16)] * 2 + [(SQUARE, jnp.float32)] * 2
    return pl.pallas_call(
        first_kernel,
        in_specs=[pl.BlockSpec(memory_space=pltpu.SMEM), vmem, vmem],
        out_specs=[hbm] * 5,
        out_shape=[jax.ShapeDtypeStruct(*shape) for shape in shapes],
        scratch_shapes=factor_scratch(6) + [pltpu.VMEM(*shape) for shape in shapes] + [pltpu.SemaphoreType.DMA((5,))],
        compiler_params=pltpu.CompilerParams(vmem_limit_bytes=60 * 1024 * 1024),
        cost_estimate=pl.CostEstimate(flops=30_000_000_000, bytes_accessed=12 << 20, transcendentals=0),
        name="first_half",
    )(place, own, other)


def second_half(place, rest, cross, mh, ml, c_turned, d_turned):
    hbm = pl.BlockSpec(memory_space=pltpu.HBM)
    arrays = (rest, cross, mh, ml, c_turned, d_turned)
    return pl.pallas_call(
        second_kernel,
        in_specs=[pl.BlockSpec(memory_space=pltpu.SMEM)] + [hbm] * 6,
        out_specs=hbm,
        out_shape=jax.ShapeDtypeStruct((256, NB), jnp.float32),
        scratch_shapes=factor_scratch(8)
        + [pltpu.VMEM(x.shape, x.dtype) for x in arrays]
        + [
            pltpu.VMEM((NB, 256), jnp.float32),
            pltpu.VMEM((256, NB), jnp.float32),
            pltpu.SemaphoreType.DMA((7,)),
        ],
        compiler_params=pltpu.CompilerParams(vmem_limit_bytes=60 * 1024 * 1024),
        cost_estimate=pl.CostEstimate(flops=1_000_000_000, bytes_accessed=6 << 20, transcendentals=0),
        name="second_half",
    )(place, *arrays)


def product_kernel(inv_ref, flags_ref, wt_ref, rows_ref, sym_ref, front_ref, child_in, out_ref, wh, wl, child_ref, sem):
    t = pl.program_id(0)

    @pl.when(t == 0)
    def _():
        pltpu.make_async_copy(child_in, child_ref, sem).start()
        high, low = split_bf16(wt_ref[...])
        wh[...] = high
        wl[...] = low

    use_sym = jnp.logical_and(flags_ref[0] == 1, t < NB // TILE)
    a = jnp.where(use_sym, sym_ref[...], rows_ref[...])
    ah, al = split_bf16(a)
    term = dot3(wh[...], wl[...], ah, al).T

    @pl.when(t == 0)
    def _():
        pltpu.make_async_copy(child_in, child_ref, sem).wait()

    keep = flags_ref[1] == 0
    for b in range(TILE // BLK):
        part = front_ref[b // 2, (b % 2) * BLK : (b % 2 + 1) * BLK, :]
        for s in range(2):
            n = inv_ref[s, (TILE // BLK) * t + b]
            part = part + jnp.where(n >= 0, child_ref[jnp.maximum(n, 0) * 2 + s], 0.0)
        part = jnp.where(keep, part, 0.0)
        out_ref[b * BLK : (b + 1) * BLK, :] = part - term[b * BLK : (b + 1) * BLK, :]


def product(inv, flags, wt, rows, sym, front, child):
    def sym_tile(t, flags):
        return jnp.where(flags[0] == 1, jnp.minimum(t, NB // TILE - 1), 0)

    return pl.pallas_call(
        product_kernel,
        grid_spec=pltpu.PrefetchScalarGridSpec(
            num_scalar_prefetch=2,
            grid=(2048 // TILE,),
            in_specs=[
                pl.BlockSpec((256, NB), lambda t, i, f: (0, 0)),
                pl.BlockSpec((NB, TILE), lambda t, i, f: (0, t)),
                pl.BlockSpec((NB, TILE), lambda t, i, f: (0, sym_tile(t, f))),
                pl.BlockSpec((TILE // 256, 256, 256), lambda t, i, f: (t, 0, 0)),
                pl.BlockSpec(memory_space=pltpu.HBM),
            ],
            out_specs=pl.BlockSpec((TILE, 256), lambda t, i, f: (t, 0)),
            scratch_shapes=[
                pltpu.VMEM((256, NB), jnp.bfloat16),
                pltpu.VMEM((256, NB), jnp.bfloat16),
                pltpu.VMEM((16, BLK, 256), jnp.float32),
                pltpu.SemaphoreType.DMA,
            ],
        ),
        out_shape=jax.ShapeDtypeStruct((2048, 256), jnp.float32),
        compiler_params=pltpu.CompilerParams(vmem_limit_bytes=60 * 1024 * 1024),
        cost_estimate=pl.CostEstimate(flops=3 * 2 * 2048 * 1024 * 256, bytes_accessed=16 << 20, transcendentals=0),
        name="product",
    )(inv, flags, wt, rows, sym, front, child)


def body(child_update, parent_front, row_map, col_map):
    half = lax.axis_index("half")
    row = lax.axis_index("row")
    col = lax.axis_index("col")
    strip = half * 8 + col
    targets = jnp.arange(W // BLK, dtype=jnp.int32)
    own_columns = lax.dynamic_index_in_dim(col_map, half, 0, keepdims=False)
    match = (own_columns[:, None] == targets[None, :]).astype(jnp.int32)
    source = jnp.sum(match * jnp.arange(8, dtype=jnp.int32)[:, None], 0)
    hit = jnp.sum(match, 0)
    rows = jnp.concatenate([row_map[:, 0] - row * 16, jnp.where(half == 0, 1, 0)[None]]).astype(jnp.int32)
    strips, wide = prep(child_update[0], parent_front, source, hit, rows)

    pieces = lax.all_to_all(strips, PLANE, 0, 0, tiled=True)
    where = pieces[1::2, 0, BLK : 3 * BLK : BLK].T.astype(jnp.int32)
    core = row % 2
    chip = (row // 2)[None]
    place = jnp.stack([core, strip]).astype(jnp.int32)
    swap = [(i, i ^ 1) for i in range(16)]
    a_strip, keep, give = assemble_strip(pieces, where, place)

    start, wanted = share(place, keep, lax.ppermute(give, "row", swap))
    halves = [lax.ppermute(start, "row", [(0, 2 * z), (1, 2 * z + 1)]) for z in range(1, 8)]
    child = lax.all_to_all(wide, PLANE, 0, 0, tiled=True)
    start, child, *halves = lax.optimization_barrier((start, child, *halves))
    spread = pick(chip, [start] + halves, copies=16)

    matching = lax.all_to_all(wanted, PLANE, 0, 0, tiled=True)
    late_strip, spread = lax.optimization_barrier((a_strip, spread))
    a_turned = lax.all_gather(late_strip, PLANE, axis=0, tiled=True)
    spread, matching = lax.optimization_barrier((spread, matching))
    gathered = lax.all_to_all(spread, PLANE, 0, 0, tiled=True)
    parent_then, _ = lax.optimization_barrier((parent_front, spread))
    turned_parent = turn(parent_then)

    def along(x, pairs):
        return lax.ppermute(x, "row", [(2 * i + n, 2 * j + n) for i, j in pairs for n in range(2)])

    mine = jnp.where(row < 2, matching, 0.0)
    to_3, to_6 = along(matching, [(0, 3)]), along(matching, [(0, 6)])
    to_3, to_6, turned_parent = lax.optimization_barrier((to_3, to_6, turned_parent))
    relay = mine + (to_3 + to_6)
    gathered, relay, turned_parent = lax.optimization_barrier((gathered, relay, turned_parent))
    other = lax.ppermute(gathered, "row", swap)
    front = lax.all_to_all(turned_parent, "col", 0, 0, tiled=True)
    last = [along(relay, [(0, 1), (3, 4), (6, 7)]), along(relay, [(3, 2), (6, 5)])]
    sym, mh, ml, rest, cross = first_half(place, gathered, other)

    rest, relay, *last = lax.optimization_barrier((rest, relay, *last))
    c_turned = relay + (last[0] + last[1])
    d_turned = lax.ppermute(c_turned, "row", swap)
    wt = second_half(place, rest, cross, mh, ml, c_turned, d_turned)

    blocks = jnp.arange(16, dtype=jnp.int32)
    order = jnp.arange(8, dtype=jnp.int32)
    inv = jnp.max(jnp.where(where[:, :, None] == blocks[None, None, :], order[None, :, None], -1), axis=1)
    flags = jnp.stack([(row == 0).astype(jnp.int32), (strip < 4).astype(jnp.int32)])
    return product(inv, flags, wt, a_turned, sym, front, child)


def solution(mesh):
    return jax.shard_map(
        body,
        mesh=mesh,
        in_specs=(
            P("half", ("row", "col"), None),
            P(("row", "col"), "half"),
            P(None, ("row", "col")),
            P(),
        ),
        out_specs=P("row", ("half", "col")),
        check_vma=False,
    )
```
